32 devices in a mesh: fsdp: 8 (over y, x, core), tp: 4 (over z).
Axes of the slice: x: 2, y: 2, z: 4, core: 2. Of those that a mesh axis runs over, the one named last changes fastest.
Arguments:
- tokens: bfloat16 [1024, 16, 2048], P('tp', 'fsdp'), may hold values from -6 to 6
- lengths: int32 [16], P('fsdp'), may hold values from 512 to 1024, as said below
- routes: int32 [1024, 16, 8], P('tp', 'fsdp'), may hold values from 0 to 15, all different within a row
- slot_order: int32 [1024, 16, 8], P('tp', 'fsdp'), may hold values from 0 to 16383, as said below
- attn_gain: float32 [2048], replicated, may hold values from 0.5 to 1.5
- query_gain: float32 [128], replicated, may hold values from 0.5 to 1.5
- key_gain: float32 [128], replicated, may hold values from 0.5 to 1.5
- query_weight: bfloat16 [2048, 2048], P('fsdp', 'tp'), may hold values from -0.125 to 0.125
- key_weight: bfloat16 [2048, 2048], P('fsdp', 'tp'), may hold values from -0.125 to 0.125
- value_weight: bfloat16 [2048, 2048], P('fsdp', 'tp'), may hold values from -0.125 to 0.125
- out_weight: bfloat16 [2048, 2048], P('tp', 'fsdp'), may hold values from -0.5 to 0.5
- moe_gain: float32 [2048], replicated, may hold values from 0.5 to 1.5
- router_weight: bfloat16 [2048, 16], P('fsdp'), may hold values from -0.0625 to 0.0625
- gate_weight: bfloat16 [16, 2048, 1024], P(None, 'fsdp', 'tp'), may hold values from -0.125 to 0.125
- up_weight: bfloat16 [16, 2048, 1024], P(None, 'fsdp', 'tp'), may hold values from -0.125 to 0.125
- down_weight: bfloat16 [16, 1024, 2048], P(None, 'tp', 'fsdp'), may hold values from -1.5 to 1.5
- cotangent: bfloat16 [1024, 16, 2048], P('tp', 'fsdp'), may hold values from -6 to 6
Outputs:
- layer_out: bfloat16 [1024, 16, 2048], P('tp', 'fsdp')
- tokens_grad: float32 [1024, 16, 2048], P('tp', 'fsdp')
- attn_gain_grad: float32 [2048], replicated
- query_gain_grad: float32 [128], replicated
- key_gain_grad: float32 [128], replicated
- query_weight_grad: float32 [2048, 2048], P('fsdp', 'tp')
- key_weight_grad: float32 [2048, 2048], P('fsdp', 'tp')
- value_weight_grad: float32 [2048, 2048], P('fsdp', 'tp')
- out_weight_grad: float32 [2048, 2048], P('tp', 'fsdp')
- moe_gain_grad: float32 [2048], replicated
- router_grad: float32 [2048, 16], P('fsdp')
- gate_grad: float32 [16, 2048, 1024], P(None, 'fsdp', 'tp')
- up_grad: float32 [16, 2048, 1024], P(None, 'fsdp', 'tp')
- down_grad: float32 [16, 1024, 2048], P(None, 'tp', 'fsdp')
The draws below stay inside these ranges and needn't reach their ends.
Inputs may be any that keep to these rules, and one draw needn't show every extreme that they name: `lengths`: in each group of 2 consecutive sequences one sequence has length 1024. `slot_order`: within each group of 2 consecutive sequences the values over all positions, sequences and choices are a permutation of 0 to 16383.
All inputs are finite; a program needn't handle non-finite values.
Results may differ from the reference program's by a relative error of at most 0.02.
Values may be sent and summed in bfloat16 or wider, within the bound.
A program may use at most 576 MiB of HBM per device.

```python
import jax
import jax.numpy as jnp
from jax import lax

D = 2048
HEADS = 16
HEAD_DIM = 128
FF = 1024
EXPERTS = 16
TOP = 8
LEN = 1024
SEQS = 2
BATCH = 16
CAP = 1280


def draw_lengths(key, part):
    groups = BATCH // SEQS
    first_key, second_key = jax.random.split(key)
    full_index = jax.random.randint(first_key, (groups,), 0, SEQS)
    other_lengths = jax.random.randint(second_key, (groups, SEQS), LEN // 2, LEN + 1)
    columns = jnp.arange(SEQS, dtype=jnp.int32)[None, :]
    shortest = (jnp.arange(groups, dtype=jnp.int32)[:, None] == 0) & (columns == (full_index[:, None] + 1) % SEQS)
    chosen = columns == full_index[:, None]
    result = jnp.where(chosen, LEN, jnp.where(shortest, LEN // 2, other_lengths))
    return result.reshape(BATCH).astype(jnp.int32)


def draw_slot_order(key, part):
    groups = BATCH // SEQS
    pair_count = LEN * SEQS * TOP
    group_keys = jax.random.split(key, groups)

    def shuffle_one(group_key):
        return jax.random.permutation(group_key, pair_count)
    shuffled = jax.vmap(shuffle_one)(group_keys).reshape(groups, LEN, SEQS, TOP)
    return jnp.moveaxis(shuffled, 0, 1).reshape(LEN, BATCH, TOP).astype(jnp.int32)


def steps_of(own_key, dims, cuts, smallest, top_value):
    level, own = 1.0, jax.random.fold_in(own_key, 6)
    for dim, blocks in cuts:
        draws = jnp.exp(jax.random.uniform(jax.random.fold_in(own, dim), (blocks,), jnp.float32, smallest / len(cuts), top_value / len(cuts)))
        level = level * jnp.repeat(draws, dims[dim] // blocks).reshape([-1 if axis == dim else 1 for axis in range(len(dims))])
    return level


def choose_distinct(rng, rows, amount, top, lift):
    order = jax.random.permutation(jax.random.fold_in(rng, 1), amount)
    favour = order
    for power in range(3):
        favour = favour * favour // amount
    favour = favour * lift // amount
    lots = jax.random.randint(jax.random.fold_in(rng, 2), (rows, amount), 0, 4096) + favour
    sure = jax.random.permutation(jax.random.fold_in(rng, 3), rows)[jnp.arange(amount) % rows]
    lots = jnp.where(jnp.arange(rows)[:, None] == sure[None, :], 1 << 14, lots)
    score = lots * amount + jnp.arange(amount)
    return lax.top_k(score.astype(jnp.int32), top)[1].astype(jnp.int32)


def centred(stream_key, dims, deviation, bound, cuts=(), kind=jnp.bfloat16):
    loudness = steps_of(stream_key, dims, cuts, -0.22, 0.18) if cuts else 1.0
    values = jax.random.normal(stream_key, dims, jnp.float32) * deviation * loudness
    return jnp.minimum(jnp.maximum(values, -bound), bound).astype(kind)


def setup_inputs(seed: int = 0) -> dict:
    key_of = jax.random.split(jax.random.key(seed), 18)
    return {
        "tokens": centred(key_of[0], (LEN, BATCH, D), 1.0, 6.0, ((0, 4), (1, 8))),
        "lengths": draw_lengths(jax.random.fold_in(key_of[17], 71), 0),
        "routes": choose_distinct(key_of[2], LEN * BATCH, EXPERTS, TOP, 4096).reshape((LEN, BATCH, TOP)),
        "slot_order": draw_slot_order(jax.random.fold_in(key_of[17], 71), 0),
        "attn_gain": jnp.clip(1.0 + 0.1 * jax.random.normal(key_of[4], (D,), jnp.float32), 0.5, 1.5),
        "query_gain": jnp.clip(1.0 + 0.1 * jax.random.normal(key_of[5], (HEAD_DIM,), jnp.float32), 0.5, 1.5),
        "key_gain": jnp.clip(1.0 + 0.1 * jax.random.normal(key_of[6], (HEAD_DIM,), jnp.float32), 0.5, 1.5),
        "query_weight": centred(key_of[7], (D, D), D ** -0.5, 0.125, ((0, 8), (1, 4))),
        "key_weight": centred(key_of[8], (D, D), D ** -0.5, 0.125, ((0, 8), (1, 4))),
        "value_weight": centred(key_of[9], (D, D), D ** -0.5, 0.125, ((0, 8), (1, 4))),
        "out_weight": centred(key_of[10], (D, D), (D // 16) ** -0.5, 0.5, ((0, 4), (1, 8))),
        "moe_gain": jnp.clip(1.0 + 0.1 * jax.random.normal(key_of[11], (D,), jnp.float32), 0.5, 1.5),
        "router_weight": centred(key_of[12], (D, EXPERTS), (4 * D) ** -0.5, 0.0625, ((0, 8),)),
        "gate_weight": centred(key_of[13], (EXPERTS, D, FF), D ** -0.5, 0.125, ((1, 8), (2, 4))),
        "up_weight": centred(key_of[14], (EXPERTS, D, FF), D ** -0.5, 0.125, ((1, 8), (2, 4))),
        "down_weight": centred(key_of[15], (EXPERTS, FF, D), (max(FF // 64, 1)) ** -0.5, 1.5, ((1, 4), (2, 8))),
        "cotangent": centred(key_of[16], (LEN, BATCH, D), 1.0, 6.0, ((0, 4), (1, 8))),
    }


EPS = 1e-06
ROPE_BASE = 10000.0
NEG_FILL = -1e+30
HIGH = lax.Precision.HIGHEST

@jax.custom_vjp
def low(v):
    return lax.optimization_barrier(v.astype(jnp.bfloat16)).astype(jnp.float32)

@jax.custom_vjp
def low_back(v):
    return v

def low_keep(v):
    return (low(v), None)

def low_pass(kept, grad):
    return (grad,)

def back_keep(v):
    return (v, None)

def back_low(kept, grad):
    return (low(grad),)
low.defvjp(low_keep, low_pass)
low_back.defvjp(back_keep, back_low)

def rms_scale(values):
    return lax.rsqrt(lax.optimization_barrier(jnp.mean(values * values, axis=-1, keepdims=True)) + EPS)

def rope_tables(length, head_width):
    half_width = head_width // 2
    frequency = ROPE_BASE ** (-(jnp.arange(half_width, dtype=jnp.float32) * 2.0 / head_width))
    angles = jnp.arange(length, dtype=jnp.float32)[:, None] * frequency[None, :]
    return (jnp.cos(angles)[:, None, None, :], jnp.sin(angles)[:, None, None, :])

def rotate(values, cosine_table, sine_table):
    half_width = values.shape[-1] // 2
    lower_half = values[..., :half_width]
    upper_half = values[..., half_width:]
    return jnp.concatenate([lower_half * cosine_table - upper_half * sine_table, lower_half * sine_table + upper_half * cosine_table], axis=-1)

def assign_slots(route_ids, order_ids, valid_rows):
    pair_count = route_ids.size
    route_flat = route_ids.reshape(-1)
    order_flat = order_ids.reshape(-1)
    valid_flat = jnp.broadcast_to(valid_rows[:, :, None], route_ids.shape).reshape(-1)
    positions = jnp.arange(pair_count, dtype=jnp.int32)
    inverse = jnp.zeros((pair_count,), jnp.int32).at[order_flat].set(positions)
    sorted_expert = route_flat[inverse]
    sorted_valid = valid_flat[inverse]
    expert_ids = jnp.arange(EXPERTS, dtype=jnp.int32)
    onehot = ((sorted_expert[:, None] == expert_ids[None, :]) & sorted_valid[:, None]).astype(jnp.int32)
    running = jnp.cumsum(onehot, axis=0).astype(jnp.int32)
    sorted_slot = lax.optimization_barrier(jnp.sum((running - 1) * onehot, axis=1)).astype(jnp.int32)
    slot_index = sorted_slot[order_flat]
    kept_pair = valid_flat & (slot_index < CAP)
    target = jnp.where(kept_pair, route_flat * CAP + slot_index, EXPERTS * CAP).astype(jnp.int32)
    token_rows = (positions // TOP).astype(jnp.int32)
    slot_rows = jnp.full((EXPERTS * CAP,), pair_count // TOP, jnp.int32).at[target].set(token_rows, mode='drop')
    return (target, slot_rows.reshape(EXPERTS, CAP))

def group_layer(group_tokens, group_lengths, group_routes, group_order, weights):
    attn_gain, query_gain, key_gain, query_weight, key_weight, value_weight, out_weight, moe_gain, router_weight, gate_weight, up_weight, down_weight = weights
    seq_count = group_tokens.shape[1]
    row_count = LEN * seq_count
    valid_rows = jnp.arange(LEN, dtype=jnp.int32)[:, None] < group_lengths[None, :]
    normed = low(group_tokens * rms_scale(group_tokens) * attn_gain)
    query_raw = low_back(jnp.einsum('psd,dh->psh', normed, query_weight, precision=HIGH)).reshape(LEN, seq_count, HEADS, HEAD_DIM)
    key_raw = low_back(jnp.einsum('psd,dh->psh', normed, key_weight, precision=HIGH)).reshape(LEN, seq_count, HEADS, HEAD_DIM)
    value_all = low(low_back(jnp.einsum('psd,dh->psh', normed, value_weight, precision=HIGH))).reshape(LEN, seq_count, HEADS, HEAD_DIM)
    cosine_table, sine_table = rope_tables(LEN, HEAD_DIM)
    query_all = low(rotate(query_raw * rms_scale(query_raw) * query_gain, cosine_table, sine_table))
    key_all = low(rotate(key_raw * rms_scale(key_raw) * key_gain, cosine_table, sine_table))
    raw_scores = jnp.einsum('qshd,kshd->shqk', query_all, key_all, precision=HIGH) * HEAD_DIM ** (-0.5)
    key_valid = jnp.transpose(valid_rows)[:, None, None, :]
    scores = low_back(jnp.where(key_valid, raw_scores, NEG_FILL))
    weights_low = low(jax.nn.softmax(scores, axis=-1))
    attended = jnp.einsum('shqk,kshd->qshd', weights_low, value_all, precision=HIGH)
    attended = low(low_back(attended)).reshape(LEN, seq_count, HEADS * HEAD_DIM)
    branch = low_back(jnp.einsum('psh,hd->psd', attended, out_weight, precision=HIGH))
    residual_sum = group_tokens + branch
    normed_two = low(residual_sum * rms_scale(residual_sum) * moe_gain)
    logits = low_back(jnp.einsum('psd,de->pse', normed_two, router_weight, precision=HIGH))
    gate_probs = jax.nn.softmax(logits, axis=-1)
    target, slot_rows = assign_slots(group_routes, group_order, valid_rows)
    token_table = jnp.concatenate([normed_two.reshape(row_count, D), jnp.zeros((1, D), jnp.float32)], axis=0)
    expert_inputs = token_table[slot_rows]
    pair_probs = jnp.take_along_axis(gate_probs, group_routes, axis=2).reshape(-1)
    slot_probs = jnp.zeros((EXPERTS * CAP,), jnp.float32).at[target].set(pair_probs, mode='drop').reshape(EXPERTS, CAP)
    gate_pre = low_back(jnp.einsum('ecd,edf->ecf', expert_inputs, gate_weight, precision=HIGH))
    up_pre = low_back(jnp.einsum('ecd,edf->ecf', expert_inputs, up_weight, precision=HIGH))
    hidden = low(jax.nn.silu(gate_pre) * up_pre)
    expert_out = low_back(jnp.einsum('ecf,efd->ecd', hidden, down_weight, precision=HIGH))
    combined = jnp.zeros((row_count + 1, D), jnp.float32).at[slot_rows].add(slot_probs[:, :, None] * expert_out)
    return residual_sum + combined[:row_count].reshape(LEN, seq_count, D)

def reference(tokens, lengths, routes, slot_order, attn_gain, query_gain, key_gain, query_weight, key_weight, value_weight, out_weight, moe_gain, router_weight, gate_weight, up_weight, down_weight, cotangent):
    groups = BATCH // SEQS

    def by_group(values):
        shaped = values.reshape((LEN, groups, SEQS) + values.shape[2:])
        return jnp.moveaxis(shaped, 1, 0)
    weights = tuple((weight_in.astype(jnp.float32) for weight_in in (attn_gain, query_gain, key_gain, query_weight, key_weight, value_weight, out_weight, moe_gain, router_weight, gate_weight, up_weight, down_weight)))
    tokens_float = tokens.astype(jnp.float32)
    valid_all = jnp.arange(LEN, dtype=jnp.int32)[:, None] < lengths[None, :]
    cot_masked = cotangent.astype(jnp.float32) * valid_all[:, :, None].astype(jnp.float32)
    integer_parts = (lengths.reshape(groups, SEQS), by_group(routes), by_group(slot_order))
    layer_check = jax.checkpoint(group_layer)

    def forward(tokens_in, weights_in):

        def one_group(parts):
            return layer_check(parts[0], parts[1], parts[2], parts[3], weights_in)
        outputs = lax.map(one_group, (by_group(tokens_in),) + integer_parts)
        return jnp.moveaxis(outputs, 0, 1).reshape(LEN, BATCH, D)
    layer_out, pullback = jax.vjp(forward, tokens_float, weights)
    tokens_grad, weight_grads = pullback(cot_masked)
    return (layer_out.astype(jnp.bfloat16), tokens_grad, weight_grads[0], weight_grads[1], weight_grads[2], weight_grads[3], weight_grads[4], weight_grads[5], weight_grads[6], weight_grads[7], weight_grads[8], weight_grads[9], weight_grads[10], weight_grads[11])
```

```python
import functools

import jax
import jax.numpy as jnp
from jax import lax
from jax.experimental import pallas as pl
from jax.experimental.pallas import tpu as pltpu
from jax.sharding import PartitionSpec as P

EXPERTS = 16
TOP = 8
CAP = 1280
LANES = 128

EPS = 1e-06
ROPE_BASE = 10000.0
NEG_FILL = -1e30
FAR = 1 << 20
BF = jnp.bfloat16
F32 = jnp.float32
VMEM_BYTES = 58 * 1024 * 1024


def dot_nn(a, b):
    return lax.dot_general(a, b, (((1,), (0,)), ((), ())), preferred_element_type=F32)


def dot_nt(a, b):
    return lax.dot_general(a, b, (((1,), (1,)), ((), ())), preferred_element_type=F32)


def dot_tn(a, b):
    return lax.dot_general(a, b, (((0,), (0,)), ((), ())), preferred_element_type=F32)


def params(steps):
    return pltpu.CompilerParams(
        dimension_semantics=("arbitrary",) * steps, vmem_limit_bytes=VMEM_BYTES
    )


def cost(macs, nbytes, exps=0):
    return pl.CostEstimate(flops=2 * macs, bytes_accessed=nbytes, transcendentals=exps)


def struct(shape, dtype):
    return jax.ShapeDtypeStruct(shape, dtype)


def rms_scale(values):
    return lax.rsqrt(jnp.mean(values * values, axis=-1, keepdims=True) + EPS)


def norm_back(grad_in, raw_values, gain_values):
    scale_rows = rms_scale(raw_values)
    normed = raw_values * scale_rows
    scaled = grad_in * gain_values
    grad_raw = scale_rows * (scaled - normed * jnp.mean(scaled * normed, axis=-1, keepdims=True))
    grad_gain = jnp.sum(grad_in * normed, axis=tuple(range(grad_in.ndim - 1)))
    return (grad_raw, grad_gain)


def shift(value, count, step):
    return lax.ppermute(value, "tp", [(i, (i + step) % count) for i in range(count)])


def ring_gather(value, count, step=1):
    held = [value]
    for _ in range(count - 1):
        held.append(shift(held[-1], count, step))
    return held


def ring_scatter(parts, step=1):
    count = len(parts)
    total = parts[1]
    for k in range(2, count + 1):
        arrived = shift(total, count, step)
        if k < count:
            total = (arrived.astype(F32) + parts[k].astype(F32)).astype(BF)
    return arrived.astype(F32) + parts[0].astype(F32)


def keep_kernel(bits, order_ref, keep_ref):
    count, experts, rows = order_ref.shape

    def below(limit):
        found = jnp.zeros((experts, 1), jnp.int32)
        for k in range(count):
            found = found + jnp.sum(
                (order_ref[k] < limit).astype(jnp.int32), axis=1, keepdims=True
            )
        return found

    last = jnp.zeros((experts, 1), jnp.int32)
    for bit in range(bits - 1, -1, -1):
        trial = last + (1 << bit)
        last = jnp.where(below(trial) < CAP, trial, last)
    for k in range(count):
        keep = (order_ref[k] <= last).astype(F32)
        wide = jnp.concatenate([keep, jnp.zeros((LANES - experts, rows), F32)], axis=0)
        keep_ref[k] = wide.T


def keep_rows(order_all, pair_count):
    count, experts, rows = order_all.shape
    return pl.pallas_call(
        functools.partial(keep_kernel, pair_count.bit_length() + 1),
        out_shape=struct((count, rows, LANES), F32),
        compiler_params=pltpu.CompilerParams(vmem_limit_bytes=VMEM_BYTES),
        cost_estimate=cost(16 * count * experts * rows, count * rows * LANES * 4),
        name="keep_rows",
    )(order_all)


def qkv_kernel(seqs, x_ref, wq_ref, wk_ref, wv_ref, cos_ref, sin_ref, gq_ref, gk_ref, *rest):
    qr_ref, kr_ref, q_ref, k_ref, v_ref = rest[-5:]
    rows = x_ref.shape[0] // seqs
    width = wq_ref.shape[1]
    heads = width // LANES
    x = x_ref[...]
    for w_ref, raw_ref, low_ref, gain_ref in (
        (wq_ref, qr_ref, q_ref, gq_ref),
        (wk_ref, kr_ref, k_ref, gk_ref),
    ):
        raw = dot_nn(x, w_ref[...])
        for s in range(seqs):
            for h in range(heads):
                part = raw[s * rows : (s + 1) * rows, h * LANES : (h + 1) * LANES]
                raw_ref[0, s, :, h * LANES : (h + 1) * LANES] = part
                normed = part * rms_scale(part) * gain_ref[...]
                turned = normed * cos_ref[0] + pltpu.roll(normed, LANES // 2, 1) * sin_ref[0]
                low_ref[0, s, :, h * LANES : (h + 1) * LANES] = turned.astype(BF)
    value = dot_nn(x, wv_ref[...]).astype(BF)
    for s in range(seqs):
        v_ref[0, s] = value[s * rows : (s + 1) * rows]


def project(k, count, seqs, x, weights, cos, sin, gain_q, gain_k, kept):
    rows, depth = x.shape
    local = (weights.shape[1] - LANES) // 3
    group = min(256, local)
    groups = local // group
    per = rows // seqs
    const = lambda *shape: pl.BlockSpec(shape, lambda g: (0,) * len(shape))
    table = pl.BlockSpec((1, per, LANES), lambda g: (k, 0, 0))
    out = pl.BlockSpec((1, seqs, per, group), lambda g: (k, 0, 0, g))
    shapes = [struct((count, seqs, per, local), d) for d in (F32, F32, BF, BF, BF)]
    aliased = list(kept or ())
    return pl.pallas_call(
        functools.partial(qkv_kernel, seqs),
        grid=(groups,),
        in_specs=[
            const(rows, depth),
            pl.BlockSpec((depth, group), lambda g: (0, g)),
            pl.BlockSpec((depth, group), lambda g: (0, groups + g)),
            pl.BlockSpec((depth, group), lambda g: (0, 2 * groups + g)),
            table,
            table,
            const(1, LANES),
            const(1, LANES),
        ]
        + [pl.BlockSpec(memory_space=pl.ANY)] * len(aliased),
        out_specs=[out] * 5,
        out_shape=shapes,
        input_output_aliases={8 + i: i for i in range(len(aliased))},
        compiler_params=params(1),
        cost_estimate=cost(rows * depth * local * 3, rows * depth * 2 + depth * local * 6),
        name="project",
    )(x, weights, weights, weights, cos, sin, gain_q, gain_k, *aliased)


def attend_kernel(scale, q_ref, k_ref, v_ref, valid_ref, o_ref, lse_ref):
    count, _, rows, width = q_ref.shape
    length = count * rows
    keys = k_ref[...].reshape(length, width)
    values_t = v_ref[...].reshape(length, width).astype(F32).T.astype(BF)
    valid = valid_ref[0][:, :1] > 0
    for i in range(count):
        scores = dot_nt(keys, q_ref[i, 0]) * scale
        weights = jnp.exp(jnp.where(valid, scores, NEG_FILL))
        total = jnp.sum(weights, axis=0, keepdims=True)
        out_t = dot_nn(values_t, weights.astype(BF)) / total
        o_ref[i, 0] = out_t.T.astype(BF)
        lse_ref[0, i : i + 1, :] = jnp.log(total)


def attend(q, k, v, valid, scale):
    count, seqs, rows, local = q.shape
    heads = local // LANES
    head = pl.BlockSpec((count, 1, rows, LANES), lambda s, h: (0, s, 0, h))
    return pl.pallas_call(
        functools.partial(attend_kernel, scale),
        grid=(seqs, heads),
        in_specs=[head, head, head, pl.BlockSpec((1, count * rows, LANES), lambda s, h: (s, 0, 0))],
        out_specs=[head, pl.BlockSpec((1, count, rows), lambda s, h: (s * heads + h, 0, 0))],
        out_shape=[struct(q.shape, BF), struct((seqs * heads, count, rows), F32)],
        compiler_params=params(2),
        cost_estimate=cost(
            2 * seqs * local * (count * rows) ** 2,
            4 * count * seqs * rows * local * 2,
            seqs * heads * (count * rows) ** 2,
        ),
        name="attend",
    )(q, k, v, valid)


def attend_back_kernel(scale, *refs):
    q_ref, k_ref, v_ref, o_ref, do_ref, lse_ref, valid_ref = refs[:7]
    qr_ref, kr_ref, cos_ref, sin_ref, gq_ref, gk_ref = refs[7:13]
    dq_ref, dk_ref, dv_ref, gains_ref = refs[13:17]
    dk_acc, dv_acc = refs[17:]
    count, _, rows, width = q_ref.shape
    length = count * rows
    first = jnp.logical_and(pl.program_id(0) == 0, pl.program_id(1) == 0)

    @pl.when(first)
    def _():
        gains_ref[...] = jnp.zeros_like(gains_ref)

    keys = k_ref[...].reshape(length, width)
    keys_t = keys.astype(F32).T.astype(BF)
    values = v_ref[...].reshape(length, width)
    valid = valid_ref[0][:, :1] > 0
    ones = jnp.ones((8, width), F32)

    def back(grad, raw, cos, sin, gain):
        turned = grad * cos - pltpu.roll(grad, LANES // 2, 1) * sin
        scale_rows = rms_scale(raw)
        normed = raw * scale_rows
        scaled = turned * gain
        mean = jnp.mean(scaled * normed, axis=-1, keepdims=True)
        return scale_rows * (scaled - normed * mean), jnp.sum(
            turned * normed, axis=0, keepdims=True
        )

    gain_q = jnp.zeros((1, width), F32)
    gain_k = jnp.zeros((1, width), F32)
    for i in range(count):
        query = q_ref[i, 0]
        grad = do_ref[i, 0]
        scores = dot_nt(keys, query) * scale
        weights = jnp.exp(jnp.where(valid, scores, NEG_FILL) - lse_ref[0, i : i + 1, :])
        delta = jnp.sum(
            (grad.astype(F32) * o_ref[i, 0].astype(F32)).T, axis=0, keepdims=True
        )
        d_weights = dot_nt(values, grad)
        d_scores = (weights * (d_weights - delta)).astype(BF)
        dv_part = dot_nn(weights.astype(BF), grad)
        dk_part = dot_nn(d_scores, query)
        if i == 0:
            dv_acc[...] = dv_part
            dk_acc[...] = dk_part
        else:
            dv_acc[...] += dv_part
            dk_acc[...] += dk_part
        dq = (dot_nn(keys_t, d_scores) * scale).T
        d_raw, d_gain = back(dq, qr_ref[i, 0], cos_ref[i], sin_ref[i], gq_ref[...])
        gain_q = gain_q + d_gain
        dq_ref[i, 0] = d_raw.astype(BF)
    for i in range(count):
        dv_ref[i, 0] = dv_acc[i * rows : (i + 1) * rows].astype(BF)
        dk = dk_acc[i * rows : (i + 1) * rows] * scale
        d_raw, d_gain = back(dk, kr_ref[i, 0], cos_ref[i], sin_ref[i], gk_ref[...])
        gain_k = gain_k + d_gain
        dk_ref[i, 0] = d_raw.astype(BF)
    gains_ref[0:1, :] += gain_q
    gains_ref[1:2, :] += gain_k


def attend_back(q, k, v, o, do, lse, valid, q_raw, k_raw, cos, sin, gain_q, gain_k, scale):
    count, seqs, rows, local = q.shape
    heads = local // LANES
    head = pl.BlockSpec((count, 1, rows, LANES), lambda s, h: (0, s, 0, h))
    const = lambda *shape: pl.BlockSpec(shape, lambda s, h: (0,) * len(shape))
    return pl.pallas_call(
        functools.partial(attend_back_kernel, scale),
        grid=(seqs, heads),
        in_specs=[
            head,
            head,
            head,
            head,
            head,
            pl.BlockSpec((1, count, rows), lambda s, h: (s * heads + h, 0, 0)),
            pl.BlockSpec((1, count * rows, LANES), lambda s, h: (s, 0, 0)),
            head,
            head,
            const(count, rows, LANES),
            const(count, rows, LANES),
            const(1, LANES),
            const(1, LANES),
        ],
        out_specs=[head, head, head, const(8, LANES)],
        out_shape=[struct(q.shape, BF)] * 3 + [struct((8, LANES), F32)],
        scratch_shapes=[pltpu.VMEM((count * rows, LANES), F32)] * 2,
        compiler_params=params(2),
        cost_estimate=cost(
            5 * seqs * local * (count * rows) ** 2,
            12 * count * seqs * rows * local * 2,
            seqs * heads * (count * rows) ** 2,
        ),
        name="attend_back",
    )(q, k, v, o, do, lse, valid, q_raw, k_raw, cos, sin, gain_q, gain_k)


def input_back_kernel(dq_ref, dk_ref, dv_ref, wq_ref, wk_ref, wv_ref, out_ref):
    total = None
    for d_ref, w_ref in ((dq_ref, wq_ref), (dk_ref, wk_ref), (dv_ref, wv_ref)):
        grad = d_ref[0].reshape(out_ref.shape[0], w_ref.shape[1])
        part = dot_nt(grad, w_ref[...])
        total = part if total is None else total + part
    out_ref[...] = total.astype(BF)


def input_back(k, dq, dk, dv, weights):
    _, seqs, per, local = dq.shape
    depth = weights.shape[0]
    rows = seqs * per
    tile = min(512, depth)
    grad = pl.BlockSpec((1, seqs, per, local), lambda t: (k, 0, 0, 0))
    return pl.pallas_call(
        input_back_kernel,
        grid=(depth // tile,),
        in_specs=[grad] * 3
        + [pl.BlockSpec((tile, local), lambda t, j=j: (t, j)) for j in range(3)],
        out_specs=pl.BlockSpec((rows, tile), lambda t: (0, t)),
        out_shape=struct((rows, depth), BF),
        compiler_params=params(1),
        cost_estimate=cost(rows * depth * local * 3, rows * depth * 2 + depth * local * 6),
        name="input_back",
    )(dq, dk, dv, weights, weights, weights)


def out_kernel(count, tok_ref, *refs):
    ob_refs = refs[:count]
    w_ref, x1_ref = refs[count:]
    local = ob_refs[0].shape[1]
    total = tok_ref[...].astype(F32)
    for s in range(count):
        total = total + dot_nn(ob_refs[s][...], w_ref[0, s * local : (s + 1) * local, :])
    x1_ref[...] = total


def out_project(tok, parts, weights):
    rows, depth = tok.shape
    blocks, full, tile = weights.shape
    count = len(parts)
    return pl.pallas_call(
        functools.partial(out_kernel, count),
        grid=(blocks,),
        in_specs=[pl.BlockSpec((rows, tile), lambda j: (0, j))]
        + [pl.BlockSpec(parts[0].shape, lambda j: (0, 0))] * count
        + [pl.BlockSpec((1, full, tile), lambda j: (j, 0, 0))],
        out_specs=pl.BlockSpec((rows, tile), lambda j: (0, j)),
        out_shape=struct((rows, depth), F32),
        compiler_params=params(1),
        cost_estimate=cost(rows * depth * full, rows * depth * 8 + full * depth * 2),
        name="out_project",
    )(tok, *parts, weights)


def out_back_kernel(db_ref, w_ref, out_ref):
    blocks, _, tile = w_ref.shape
    total = None
    for j in range(blocks):
        part = dot_nt(db_ref[:, j * tile : (j + 1) * tile], w_ref[j])
        total = part if total is None else total + part
    out_ref[0] = total.astype(BF)


def out_back(db, weights, count):
    rows, depth = db.shape
    blocks, full, tile = weights.shape
    local = full // count
    return pl.pallas_call(
        out_back_kernel,
        grid=(count,),
        in_specs=[
            pl.BlockSpec((rows, depth), lambda s: (0, 0)),
            pl.BlockSpec((blocks, local, tile), lambda s: (0, s, 0)),
        ],
        out_specs=pl.BlockSpec((1, rows, local), lambda s: (s, 0, 0)),
        out_shape=struct((count, rows, local), BF),
        compiler_params=params(1),
        cost_estimate=cost(rows * depth * full, rows * depth * 2 + full * depth * 2),
        name="out_back",
    )(db, weights)


def expert_kernel(n2_ref, c_ref, keep_ref, router_ref, g_ref, u_ref, d_ref, *rest):
    hp_ref, da_ref, du_ref, y_ref, dn_ref, dl_ref = rest[-12:-6]
    probs, gates, grads, y_acc, dn_acc, d_full = rest[-6:]
    e = pl.program_id(0)
    experts = pl.num_programs(0)
    blocks, _, _, tile = d_ref.shape
    rows = n2_ref.shape[0]
    lane = lax.broadcasted_iota(jnp.int32, (rows, LANES), 1)

    @pl.when(e == 0)
    def _():
        logits = jnp.where(lane < EXPERTS, dot_nn(n2_ref[...], router_ref[...]), NEG_FILL)
        raised = jnp.exp(logits - jnp.max(logits, axis=-1, keepdims=True))
        soft = raised / jnp.sum(raised, axis=-1, keepdims=True)
        probs[...] = soft
        gates[...] = soft * keep_ref[0]
        grads[...] = jnp.zeros_like(grads)

    for j in range(blocks):
        d_full[:, j * tile : (j + 1) * tile] = d_ref[j, 0]
    here = lane == e
    gate = jnp.sum(jnp.where(here, gates[...], 0.0), axis=-1, keepdims=True)
    x = n2_ref[...]
    pre = dot_nn(x, g_ref[0])
    up = dot_nn(x, u_ref[0])
    back = dot_nt(c_ref[...], d_full[...])
    sig = 1.0 / (1.0 + jnp.exp(-pre))
    act = pre * sig
    hid = act * up
    hp = (hid * gate).astype(BF)
    column = jnp.sum(back * hid, axis=-1, keepdims=True)
    grads[...] += jnp.where(here, column * keep_ref[0], 0.0)
    dh = back * gate
    du = (dh * act).astype(BF)
    da = (dh * up * (sig + act * (1.0 - sig))).astype(BF)
    hp_ref[0] = hp
    da_ref[0] = da
    du_ref[0] = du
    y_part = dot_nn(hp, d_full[...])
    dn_part = dot_nt(da, g_ref[0]) + dot_nt(du, u_ref[0])

    @pl.when(e == 0)
    def _():
        y_acc[...] = y_part
        dn_acc[...] = dn_part

    @pl.when(e > 0)
    def _():
        y_acc[...] += y_part
        dn_acc[...] += dn_part

    @pl.when(e == experts - 1)
    def _():
        soft = probs[...]
        gd = grads[...]
        dl = (soft * (gd - jnp.sum(soft * gd, axis=-1, keepdims=True))).astype(BF)
        dl_ref[0] = dl
        y_ref[...] = y_acc[...].astype(BF)
        dn_ref[...] = (dn_acc[...] + dot_nt(dl, router_ref[...])).astype(BF)


def experts_pass(k, count, n2, cot, keep, weights_all, gate_w, up_w, down_w, kept):
    rows, depth = n2.shape
    experts, _, ff = gate_w.shape
    blocks, _, _, tile = down_w.shape
    router_col = weights_all.shape[1] // LANES - 1
    const = lambda *shape: pl.BlockSpec(shape, lambda e: (0,) * len(shape))
    wide = pl.BlockSpec((1, rows, ff), lambda e: (k, 0, e))
    aliased = list(kept or ())
    return pl.pallas_call(
        expert_kernel,
        grid=(experts,),
        in_specs=[
            const(rows, depth),
            const(rows, depth),
            pl.BlockSpec((1, rows, LANES), lambda e: (k, 0, 0)),
            pl.BlockSpec((depth, LANES), lambda e: (0, router_col)),
            pl.BlockSpec((1, depth, ff), lambda e: (e, 0, 0)),
            pl.BlockSpec((1, depth, ff), lambda e: (e, 0, 0)),
            pl.BlockSpec((blocks, 1, ff, tile), lambda e: (0, e, 0, 0)),
        ]
        + [pl.BlockSpec(memory_space=pl.ANY)] * len(aliased),
        out_specs=[
            wide,
            wide,
            wide,
            const(rows, depth),
            const(rows, depth),
            pl.BlockSpec((1, rows, LANES), lambda e: (k, 0, 0)),
        ],
        out_shape=[struct((count, rows, experts * ff), BF)] * 3
        + [struct((rows, depth), BF)] * 2
        + [struct((count, rows, LANES), BF)],
        input_output_aliases=dict(zip(range(7, 11), (0, 1, 2, 5))) if aliased else {},
        scratch_shapes=[
            pltpu.VMEM((rows, LANES), F32),
            pltpu.VMEM((rows, LANES), F32),
            pltpu.VMEM((rows, LANES), F32),
            pltpu.VMEM((rows, depth), F32),
            pltpu.VMEM((rows, depth), F32),
            pltpu.VMEM((ff, depth), BF),
        ],
        compiler_params=params(1),
        cost_estimate=cost(
            6 * rows * depth * ff * experts,
            3 * experts * depth * ff * 2 + 4 * rows * depth * 2 + 3 * rows * experts * ff * 2,
            2 * rows * ff * experts,
        ),
        name="experts",
    )(n2, cot, keep, weights_all, gate_w, up_w, down_w, *aliased)


def per_device(
    tokens,
    lengths,
    routes,
    slot_order,
    attn_gain,
    query_gain,
    key_gain,
    query_weight,
    key_weight,
    value_weight,
    out_weight,
    moe_gain,
    router_weight,
    gate_weight,
    up_weight,
    down_weight,
    cotangent,
):
    per, seqs, depth = tokens.shape
    count = lax.axis_size("tp")
    me = lax.axis_index("tp")
    length = per * count
    rows = seqs * per
    head_width = query_gain.shape[0]
    local = query_weight.shape[1]
    scale = head_width ** (-0.5)

    first = jnp.concatenate(
        [
            query_weight,
            key_weight,
            value_weight,
            jnp.pad(router_weight, ((0, 0), (0, LANES - EXPERTS))),
        ],
        axis=1,
    )
    weights_all = lax.all_gather(first, "fsdp", axis=0, tiled=True)

    tok = jnp.transpose(tokens, (1, 0, 2)).reshape(rows, depth)
    tok_float = tok.astype(F32)
    n1_own = (tok_float * rms_scale(tok_float) * attn_gain).astype(BF)
    n1 = ring_gather(n1_own, count)

    out_rows = jnp.concatenate(ring_gather(out_weight, count, -1), axis=0)
    out_all = lax.all_gather(out_rows, "fsdp", axis=0, tiled=False)
    gate_all = lax.all_gather(gate_weight, "fsdp", axis=1, tiled=True)
    up_all = lax.all_gather(up_weight, "fsdp", axis=1, tiled=True)
    down_all = lax.all_gather(down_weight, "fsdp", axis=0, tiled=False)

    own_pos = me * per + jnp.arange(per, dtype=jnp.int32)
    valid_own = own_pos[None, :] < lengths[:, None]
    route_t = jnp.transpose(routes, (2, 1, 0)).reshape(TOP, rows)
    order_t = jnp.transpose(slot_order, (2, 1, 0)).reshape(TOP, rows)
    names = jnp.arange(EXPERTS, dtype=jnp.int32)[:, None]
    order_own = jnp.full((EXPERTS, rows), FAR, jnp.int32)
    for j in range(TOP):
        order_own = jnp.where(route_t[j][None, :] == names, order_t[j][None, :], order_own)
    order_own = jnp.where(valid_own.reshape(1, rows), order_own, FAR)
    order_all = jnp.stack(ring_gather(order_own, count))
    keep = keep_rows(order_all, length * seqs * TOP)

    owner = (me - jnp.arange(count, dtype=jnp.int32)) % count
    chunk_pos = owner[:, None] * per + jnp.arange(per, dtype=jnp.int32)[None, :]
    half = head_width // 2
    frequency = ROPE_BASE ** (-(jnp.arange(half, dtype=F32) * 2.0 / head_width))
    angles = chunk_pos.astype(F32)[:, :, None] * frequency
    cos_half, sin_half = jnp.cos(angles), jnp.sin(angles)
    cos = jnp.concatenate([cos_half, cos_half], axis=-1)
    sin = jnp.concatenate([-sin_half, sin_half], axis=-1)
    key_valid = (chunk_pos.reshape(1, length) < lengths[:, None]).astype(F32)
    key_valid = jnp.broadcast_to(key_valid[:, :, None], (seqs, length, LANES))

    gain_q, gain_k = query_gain[None, :], key_gain[None, :]
    kept = None
    for k in range(count):
        kept = project(k, count, seqs, n1[k], weights_all, cos, sin, gain_q, gain_k, kept)
    q_raw, k_raw, q, k_low, v = kept

    cot = jnp.transpose(cotangent, (1, 0, 2)).reshape(rows, depth)
    cot_own = jnp.where(valid_own.reshape(rows, 1), cot, jnp.zeros_like(cot))
    cot_own, _ = lax.optimization_barrier((cot_own, n1[-1]))
    cots = ring_gather(cot_own, count)

    ob, lse = attend(q, k_low, v, key_valid, scale)
    ob_rows = ob.reshape(count, rows, local)
    ob_parts = [ob_rows[0]] + [shift(ob_rows[s], count, -s) for s in range(1, count)]
    x1 = out_project(tok, ob_parts, out_all)
    n2_own = (x1 * rms_scale(x1) * moe_gain).astype(BF)
    n2 = ring_gather(n2_own, count)

    kept = None
    y_parts, dn_parts = [], []
    for k in range(count):
        hp, da, du, y_k, dn_k, dl = experts_pass(
            k, count, n2[k], cots[k], keep, weights_all, gate_all, up_all, down_all, kept
        )
        kept = (hp, da, du, dl)
        y_parts.append(y_k)
        dn_parts.append(dn_k)
    dn2 = ring_scatter(dn_parts)

    n2_all = jnp.concatenate(n2, axis=0)
    cot_all = jnp.concatenate(cots, axis=0)
    all_rows = count * rows
    ff = gate_weight.shape[2]

    def expert_grad(left, right):
        full = dot_tn(left, right.reshape(all_rows, EXPERTS * ff)).astype(BF)
        own = lax.psum_scatter(full, "fsdp", scatter_dimension=0, tiled=True)
        return own.reshape(own.shape[0], EXPERTS, ff)

    gate_grad = jnp.transpose(expert_grad(n2_all, da), (1, 0, 2)).astype(F32)
    up_grad = jnp.transpose(expert_grad(n2_all, du), (1, 0, 2)).astype(F32)
    down_grad = jnp.transpose(expert_grad(cot_all, hp), (1, 2, 0)).astype(F32)
    router_term = dot_tn(n2_all, dl.reshape(all_rows, LANES))[:, :EXPERTS]

    moe_back, moe_gain_term = norm_back(dn2, x1, moe_gain)
    dx1 = moe_back + cot_own.astype(F32)
    db = dx1.astype(BF)
    dob = out_back(db, out_all, count)
    dob_parts = [dob[0]] + [shift(dob[s], count, s) for s in range(1, count)]
    d_ob = jnp.stack(dob_parts).reshape(count, seqs, per, local)

    y_sum = ring_scatter(y_parts)
    layer_out = (x1 + y_sum).astype(BF)

    ob_cat = jnp.concatenate(ob_parts, axis=1)
    out_full = dot_tn(db, ob_cat).astype(BF)
    out_sum = lax.psum_scatter(out_full, "fsdp", scatter_dimension=0, tiled=True)
    out_pieces = [out_sum[:, s * local : (s + 1) * local] for s in range(count)]
    out_weight_grad = jnp.transpose(ring_scatter(out_pieces, -1))

    dq, dk, dv, gains = attend_back(
        q, k_low, v, ob, d_ob, lse, key_valid, q_raw, k_raw, cos, sin, gain_q, gain_k, scale
    )
    dn1_parts = [None] * count
    for k in list(range(1, count)) + [0]:
        dn1_parts[k] = input_back(k, dq, dk, dv, weights_all)
    dn1 = ring_scatter(dn1_parts)
    n1_all = jnp.concatenate(n1, axis=0)
    d_all = jnp.concatenate([d.reshape(all_rows, local) for d in (dq, dk, dv)], axis=1)
    qkv_full = dot_tn(n1_all, d_all).astype(BF)
    qkv_sum = lax.psum_scatter(qkv_full, "fsdp", scatter_dimension=0, tiled=True).astype(F32)

    attn_back, attn_gain_term = norm_back(dn1, tok_float, attn_gain)
    tokens_grad = attn_back + dx1

    small = lax.psum(
        (attn_gain_term, gains[0], gains[1], moe_gain_term, router_term), ("fsdp", "tp")
    )
    router_rows = depth // lax.axis_size("fsdp")
    router_grad = lax.dynamic_slice_in_dim(
        small[4], lax.axis_index("fsdp") * router_rows, router_rows, 0
    )

    def back_to_positions(value):
        return jnp.transpose(value.reshape(seqs, per, depth), (1, 0, 2))

    return (
        back_to_positions(layer_out),
        back_to_positions(tokens_grad),
        small[0],
        small[1],
        small[2],
        qkv_sum[:, :local],
        qkv_sum[:, local : 2 * local],
        qkv_sum[:, 2 * local :],
        out_weight_grad,
        small[3],
        router_grad,
        gate_grad,
        up_grad,
        down_grad,
    )


def solution(mesh):
    return jax.shard_map(
        per_device,
        mesh=mesh,
        in_specs=(
            P("tp", "fsdp", None),
            P("fsdp"),
            P("tp", "fsdp", None),
            P("tp", "fsdp", None),
            P(),
            P(),
            P(),
            P("fsdp", "tp"),
            P("fsdp", "tp"),
            P("fsdp", "tp"),
            P("tp", "fsdp"),
            P(),
            P("fsdp", None),
            P(None, "fsdp", "tp"),
            P(None, "fsdp", "tp"),
            P(None, "tp", "fsdp"),
            P("tp", "fsdp", None),
        ),
        out_specs=(
            P("tp", "fsdp", None),
            P("tp", "fsdp", None),
            P(),
            P(),
            P(),
            P("fsdp", "tp"),
            P("fsdp", "tp"),
            P("fsdp", "tp"),
            P("tp", "fsdp"),
            P(),
            P("fsdp", None),
            P(None, "fsdp", "tp"),
            P(None, "fsdp", "tp"),
            P(None, "tp", "fsdp"),
        ),
        check_vma=False,
    )
```

```python
import functools

import jax
import jax.numpy as jnp
from jax import lax
from jax.experimental import pallas as pl
from jax.experimental.pallas import tpu as pltpu
from jax.sharding import PartitionSpec as P

EXPERTS = 16
TOP = 8
CAP = 1280
LANES = 128

EPS = 1e-06
ROPE_BASE = 10000.0
NEG_FILL = -1e30
FAR = 1 << 20
BF = jnp.bfloat16
F32 = jnp.float32
VMEM_BYTES = 58 * 1024 * 1024
GROUPS = 2


def dot_nn(a, b):
    return lax.dot_general(a, b, (((1,), (0,)), ((), ())), preferred_element_type=F32)


def dot_nt(a, b):
    return lax.dot_general(a, b, (((1,), (1,)), ((), ())), preferred_element_type=F32)


def dot_tn(a, b):
    return lax.dot_general(a, b, (((0,), (0,)), ((), ())), preferred_element_type=F32)


def params(steps):
    return pltpu.CompilerParams(
        dimension_semantics=("arbitrary",) * steps, vmem_limit_bytes=VMEM_BYTES
    )


def cost(macs, nbytes, exps=0):
    return pl.CostEstimate(flops=32 * macs, bytes_accessed=nbytes, transcendentals=exps)


def struct(shape, dtype):
    return jax.ShapeDtypeStruct(shape, dtype)


def rms_scale(values):
    return lax.rsqrt(jnp.mean(values * values, axis=-1, keepdims=True) + EPS)


def norm_back(grad_in, raw_values, gain_values):
    scale_rows = rms_scale(raw_values)
    normed = raw_values * scale_rows
    scaled = grad_in * gain_values
    grad_raw = scale_rows * (scaled - normed * jnp.mean(scaled * normed, axis=-1, keepdims=True))
    grad_gain = jnp.sum(grad_in * normed, axis=tuple(range(grad_in.ndim - 1)))
    return (grad_raw, grad_gain)


def shift(value, count, step):
    return lax.ppermute(value, "tp", [(i, (i + step) % count) for i in range(count)])


def after(value, *done):
    return lax.optimization_barrier((value,) + done)[0]


def ring_gather(value, count, step=1):
    held = [value]
    for _ in range(count - 1):
        held.append(shift(held[-1], count, step))
    return held


def plus(arrived, *parts):
    total = arrived.astype(F32)
    for part in parts:
        total = total + part.astype(F32)
    return total


def ring_scatter(parts, step=1):
    count = len(parts)
    total = parts[1]
    for k in range(2, count + 1):
        arrived = shift(total, count, step)
        if k < count:
            total = plus(arrived, parts[k]).astype(BF)
    return plus(arrived, parts[0])


def keep_kernel(bits, order_ref, keep_ref):
    count, experts, rows = order_ref.shape

    def below(limit):
        found = jnp.zeros((experts, 1), jnp.int32)
        for k in range(count):
            found = found + jnp.sum(
                (order_ref[k] < limit).astype(jnp.int32), axis=1, keepdims=True
            )
        return found

    last = jnp.zeros((experts, 1), jnp.int32)
    for bit in range(bits - 1, -1, -1):
        trial = last + (1 << bit)
        last = jnp.where(below(trial) < CAP, trial, last)
    for k in range(count):
        keep = (order_ref[k] <= last).astype(F32)
        wide = jnp.concatenate([keep, jnp.zeros((LANES - experts, rows), F32)], axis=0)
        keep_ref[k] = wide.T


def keep_rows(order_all, pair_count):
    count, experts, rows = order_all.shape
    return pl.pallas_call(
        functools.partial(keep_kernel, pair_count.bit_length() + 1),
        out_shape=struct((count, rows, LANES), F32),
        compiler_params=pltpu.CompilerParams(vmem_limit_bytes=VMEM_BYTES),
        cost_estimate=cost(16 * count * experts * rows, count * rows * LANES * 4),
        name="keep_rows",
    )(order_all)


def qkv_kernel(seqs, x_ref, wq_ref, wk_ref, wv_ref, cos_ref, sin_ref, gq_ref, gk_ref, *rest):
    qr_ref, kr_ref, q_ref, k_ref, v_ref = rest[-5:]
    rows = x_ref.shape[0] // seqs
    width = wq_ref.shape[1]
    heads = width // LANES
    x = x_ref[...]
    for w_ref, raw_ref, low_ref, gain_ref in (
        (wq_ref, qr_ref, q_ref, gq_ref),
        (wk_ref, kr_ref, k_ref, gk_ref),
    ):
        raw = dot_nn(x, w_ref[...])
        for s in range(seqs):
            for h in range(heads):
                part = raw[s * rows : (s + 1) * rows, h * LANES : (h + 1) * LANES]
                raw_ref[0, s, :, h * LANES : (h + 1) * LANES] = part
                normed = part * rms_scale(part) * gain_ref[...]
                turned = normed * cos_ref[0] + pltpu.roll(normed, LANES // 2, 1) * sin_ref[0]
                low_ref[0, s, :, h * LANES : (h + 1) * LANES] = turned.astype(BF)
    value = dot_nn(x, wv_ref[...]).astype(BF)
    for s in range(seqs):
        v_ref[0, s] = value[s * rows : (s + 1) * rows]


def project(k, count, seqs, x, weights, cos, sin, gain_q, gain_k, kept):
    rows, depth = x.shape
    local = (weights.shape[1] - LANES) // 3
    group = min(256, local)
    groups = local // group
    per = rows // seqs
    const = lambda *shape: pl.BlockSpec(shape, lambda g: (0,) * len(shape))
    table = pl.BlockSpec((1, per, LANES), lambda g: (k, 0, 0))
    out = pl.BlockSpec((1, seqs, per, group), lambda g: (k, 0, 0, g))
    shapes = [struct((count, seqs, per, local), d) for d in (F32, F32, BF, BF, BF)]
    aliased = list(kept or ())
    return pl.pallas_call(
        functools.partial(qkv_kernel, seqs),
        grid=(groups,),
        in_specs=[
            const(rows, depth),
            pl.BlockSpec((depth, group), lambda g: (0, g)),
            pl.BlockSpec((depth, group), lambda g: (0, groups + g)),
            pl.BlockSpec((depth, group), lambda g: (0, 2 * groups + g)),
            table,
            table,
            const(1, LANES),
            const(1, LANES),
        ]
        + [pl.BlockSpec(memory_space=pl.ANY)] * len(aliased),
        out_specs=[out] * 5,
        out_shape=shapes,
        input_output_aliases={8 + i: i for i in range(len(aliased))},
        compiler_params=params(1),
        cost_estimate=cost(rows * depth * local * 3, rows * depth * 2 + depth * local * 6),
        name="project",
    )(x, weights, weights, weights, cos, sin, gain_q, gain_k, *aliased)


def attend_kernel(scale, q_ref, k_ref, v_ref, valid_ref, o_ref, lse_ref):
    count, _, rows, width = q_ref.shape
    length = count * rows
    keys = k_ref[...].reshape(length, width)
    values_t = v_ref[...].reshape(length, width).astype(F32).T.astype(BF)
    valid = valid_ref[0][:, :1] > 0
    for i in range(count):
        scores = dot_nt(keys, q_ref[i, 0]) * scale
        weights = jnp.exp(jnp.where(valid, scores, NEG_FILL))
        total = jnp.sum(weights, axis=0, keepdims=True)
        out_t = dot_nn(values_t, weights.astype(BF)) / total
        o_ref[i, 0] = out_t.T.astype(BF)
        lse_ref[0, i : i + 1, :] = jnp.log(total)


def attend(q, k, v, valid, scale):
    count, seqs, rows, local = q.shape
    heads = local // LANES
    head = pl.BlockSpec((count, 1, rows, LANES), lambda s, h: (0, s, 0, h))
    return pl.pallas_call(
        functools.partial(attend_kernel, scale),
        grid=(seqs, heads),
        in_specs=[head, head, head, pl.BlockSpec((1, count * rows, LANES), lambda s, h: (s, 0, 0))],
        out_specs=[head, pl.BlockSpec((1, count, rows), lambda s, h: (s * heads + h, 0, 0))],
        out_shape=[struct(q.shape, BF), struct((seqs * heads, count, rows), F32)],
        compiler_params=params(2),
        cost_estimate=cost(
            2 * seqs * local * (count * rows) ** 2,
            4 * count * seqs * rows * local * 2,
            seqs * heads * (count * rows) ** 2,
        ),
        name="attend",
    )(q, k, v, valid)


def attend_back_kernel(scale, *refs):
    q_ref, k_ref, v_ref, o_ref, do_ref, lse_ref, valid_ref = refs[:7]
    qr_ref, kr_ref, cos_ref, sin_ref, gq_ref, gk_ref = refs[7:13]
    dq_ref, dk_ref, dv_ref, gains_ref = refs[13:17]
    dk_acc, dv_acc = refs[17:]
    count, _, rows, width = q_ref.shape
    length = count * rows
    first = jnp.logical_and(pl.program_id(0) == 0, pl.program_id(1) == 0)

    @pl.when(first)
    def _():
        gains_ref[...] = jnp.zeros_like(gains_ref)

    keys = k_ref[...].reshape(length, width)
    keys_t = keys.astype(F32).T.astype(BF)
    values = v_ref[...].reshape(length, width)
    valid = valid_ref[0][:, :1] > 0
    ones = jnp.ones((8, width), F32)

    def back(grad, raw, cos, sin, gain):
        turned = grad * cos - pltpu.roll(grad, LANES // 2, 1) * sin
        scale_rows = rms_scale(raw)
        normed = raw * scale_rows
        scaled = turned * gain
        mean = jnp.mean(scaled * normed, axis=-1, keepdims=True)
        return scale_rows * (scaled - normed * mean), jnp.sum(
            turned * normed, axis=0, keepdims=True
        )

    gain_q = jnp.zeros((1, width), F32)
    gain_k = jnp.zeros((1, width), F32)
    for i in range(count):
        query = q_ref[i, 0]
        grad = do_ref[i, 0]
        scores = dot_nt(keys, query) * scale
        weights = jnp.exp(jnp.where(valid, scores, NEG_FILL) - lse_ref[0, i : i + 1, :])
        delta = jnp.sum(
            (grad.astype(F32) * o_ref[i, 0].astype(F32)).T, axis=0, keepdims=True
        )
        d_weights = dot_nt(values, grad)
        d_scores = (weights * (d_weights - delta)).astype(BF)
        dv_part = dot_nn(weights.astype(BF), grad)
        dk_part = dot_nn(d_scores, query)
        if i == 0:
            dv_acc[...] = dv_part
            dk_acc[...] = dk_part
        else:
            dv_acc[...] += dv_part
            dk_acc[...] += dk_part
        dq = (dot_nn(keys_t, d_scores) * scale).T
        d_raw, d_gain = back(dq, qr_ref[i, 0], cos_ref[i], sin_ref[i], gq_ref[...])
        gain_q = gain_q + d_gain
        dq_ref[i, 0] = d_raw.astype(BF)
    for i in range(count):
        dv_ref[i, 0] = dv_acc[i * rows : (i + 1) * rows].astype(BF)
        dk = dk_acc[i * rows : (i + 1) * rows] * scale
        d_raw, d_gain = back(dk, kr_ref[i, 0], cos_ref[i], sin_ref[i], gk_ref[...])
        gain_k = gain_k + d_gain
        dk_ref[i, 0] = d_raw.astype(BF)
    gains_ref[0:1, :] += gain_q
    gains_ref[1:2, :] += gain_k


def attend_back(q, k, v, o, do, lse, valid, q_raw, k_raw, cos, sin, gain_q, gain_k, scale):
    count, seqs, rows, local = q.shape
    heads = local // LANES
    head = pl.BlockSpec((count, 1, rows, LANES), lambda s, h: (0, s, 0, h))
    const = lambda *shape: pl.BlockSpec(shape, lambda s, h: (0,) * len(shape))
    return pl.pallas_call(
        functools.partial(attend_back_kernel, scale),
        grid=(seqs, heads),
        in_specs=[
            head,
            head,
            head,
            head,
            head,
            pl.BlockSpec((1, count, rows), lambda s, h: (s * heads + h, 0, 0)),
            pl.BlockSpec((1, count * rows, LANES), lambda s, h: (s, 0, 0)),
            head,
            head,
            const(count, rows, LANES),
            const(count, rows, LANES),
            const(1, LANES),
            const(1, LANES),
        ],
        out_specs=[head, head, head, const(8, LANES)],
        out_shape=[struct(q.shape, BF)] * 3 + [struct((8, LANES), F32)],
        scratch_shapes=[pltpu.VMEM((count * rows, LANES), F32)] * 2,
        compiler_params=params(2),
        cost_estimate=cost(
            5 * seqs * local * (count * rows) ** 2,
            12 * count * seqs * rows * local * 2,
            seqs * heads * (count * rows) ** 2,
        ),
        name="attend_back",
    )(q, k, v, o, do, lse, valid, q_raw, k_raw, cos, sin, gain_q, gain_k)


def input_back_kernel(dq_ref, dk_ref, dv_ref, wq_ref, wk_ref, wv_ref, out_ref):
    total = None
    for d_ref, w_ref in ((dq_ref, wq_ref), (dk_ref, wk_ref), (dv_ref, wv_ref)):
        grad = d_ref[0].reshape(out_ref.shape[0], w_ref.shape[1])
        part = dot_nt(grad, w_ref[...])
        total = part if total is None else total + part
    out_ref[...] = total.astype(BF)


def input_back(k, dq, dk, dv, weights):
    _, seqs, per, local = dq.shape
    depth = weights.shape[0]
    rows = seqs * per
    tile = min(512, depth)
    grad = pl.BlockSpec((1, seqs, per, local), lambda t: (k, 0, 0, 0))
    return pl.pallas_call(
        input_back_kernel,
        grid=(depth // tile,),
        in_specs=[grad] * 3
        + [pl.BlockSpec((tile, local), lambda t, j=j: (t, j)) for j in range(3)],
        out_specs=pl.BlockSpec((rows, tile), lambda t: (0, t)),
        out_shape=struct((rows, depth), BF),
        compiler_params=params(1),
        cost_estimate=cost(rows * depth * local * 3 // 16, rows * depth * 2 + depth * local * 6),
        name="input_back",
    )(dq, dk, dv, weights, weights, weights)


def out_kernel(count, tok_ref, *refs):
    ob_refs = refs[:count]
    w_ref, x1_ref = refs[count:]
    local = ob_refs[0].shape[1]
    total = tok_ref[...].astype(F32)
    for s in range(count):
        total = total + dot_nn(ob_refs[s][...], w_ref[0, s * local : (s + 1) * local, :])
    x1_ref[...] = total


def out_project(tok, parts, weights):
    rows, depth = tok.shape
    blocks, full, tile = weights.shape
    count = len(parts)
    return pl.pallas_call(
        functools.partial(out_kernel, count),
        grid=(blocks,),
        in_specs=[pl.BlockSpec((rows, tile), lambda j: (0, j))]
        + [pl.BlockSpec(parts[0].shape, lambda j: (0, 0))] * count
        + [pl.BlockSpec((1, full, tile), lambda j: (j, 0, 0))],
        out_specs=pl.BlockSpec((rows, tile), lambda j: (0, j)),
        out_shape=struct((rows, depth), F32),
        compiler_params=params(1),
        cost_estimate=cost(rows * depth * full, rows * depth * 8 + full * depth * 2),
        name="out_project",
    )(tok, *parts, weights)


def out_back_kernel(db_ref, w_ref, out_ref):
    blocks, _, tile = w_ref.shape
    total = None
    for j in range(blocks):
        part = dot_nt(db_ref[:, j * tile : (j + 1) * tile], w_ref[j])
        total = part if total is None else total + part
    out_ref[0] = total.astype(BF)


def out_back(db, weights, count):
    rows, depth = db.shape
    blocks, full, tile = weights.shape
    local = full // count
    return pl.pallas_call(
        out_back_kernel,
        grid=(count,),
        in_specs=[
            pl.BlockSpec((rows, depth), lambda s: (0, 0)),
            pl.BlockSpec((blocks, local, tile), lambda s: (0, s, 0)),
        ],
        out_specs=pl.BlockSpec((1, rows, local), lambda s: (s, 0, 0)),
        out_shape=struct((count, rows, local), BF),
        compiler_params=params(1),
        cost_estimate=cost(rows * depth * full, rows * depth * 2 + full * depth * 2),
        name="out_back",
    )(db, weights)


def expert_kernel(group, experts, n2_ref, c_ref, keep_ref, router_ref, tile_ref, w_ref, *rest):
    last = group == GROUPS - 1
    wt_ref, grad_in = rest[0], rest[1]
    hp_ref, da_ref, du_ref, y_ref, dn_ref, grad_out = rest[-14:-8]
    probs, gates, grads, hp_all, da_all, du_all, full, low = rest[-8:]
    e = pl.program_id(0)
    blocks, _, _, ff, tile = w_ref.shape
    rows = n2_ref.shape[0]
    lane = lax.broadcasted_iota(jnp.int32, (rows, LANES), 1)

    @pl.when(e == 0)
    def _():
        logits = jnp.where(lane < EXPERTS, dot_nn(n2_ref[...], router_ref[...]), NEG_FILL)
        raised = jnp.exp(logits - jnp.max(logits, axis=-1, keepdims=True))
        soft = raised / jnp.sum(raised, axis=-1, keepdims=True)
        probs[...] = soft
        gates[...] = soft * keep_ref[0]
        grads[...] = jnp.zeros_like(grads) if group == 0 else grad_in[...]

    @pl.when(e < experts)
    def _():
        for t in range(3):
            for j in range(blocks):
                full[t, :, j * tile : (j + 1) * tile] = w_ref[j, t, 0]
        here = lane == e + group * experts
        gate = jnp.sum(jnp.where(here, gates[...], 0.0), axis=-1, keepdims=True)
        x = n2_ref[...]
        pre = dot_nt(x, full[0])
        up = dot_nt(x, full[1])
        back = dot_nt(c_ref[...], full[2])
        sig = 1.0 / (1.0 + jnp.exp(-pre))
        act = pre * sig
        hid = act * up
        hp = (hid * gate).astype(BF)
        column = jnp.sum(back * hid, axis=-1, keepdims=True)
        grads[...] += jnp.where(here, column * keep_ref[0], 0.0)
        dh = back * gate
        du = (dh * act).astype(BF)
        da = (dh * up * (sig + act * (1.0 - sig))).astype(BF)
        hp_ref[0] = hp
        da_ref[0] = da
        du_ref[0] = du
        place = pl.ds(pl.multiple_of(e * ff, ff), ff)
        hp_all[:, place] = hp
        da_all[:, place] = da
        du_all[:, place] = du

    @pl.when(e == experts - 1)
    def _():
        if last:
            soft = probs[...]
            gd = grads[...]
            dl = (soft * (gd - jnp.sum(soft * gd, axis=-1, keepdims=True))).astype(BF)
            grad_out[...] = dl
            low[...] = dl
        else:
            grad_out[...] = grads[...]

    @pl.when(e >= experts)
    def _():
        wide = experts * ff
        y_ref[...] = dot_nn(hp_all[...], wt_ref[0, 2].reshape(wide, tile)).astype(BF)
        total = dot_nn(da_all[...], wt_ref[0, 0].reshape(wide, tile))
        total = total + dot_nn(du_all[...], wt_ref[0, 1].reshape(wide, tile))
        if last:
            total = total + dot_nt(low[...], tile_ref[...])
        dn_ref[...] = total.astype(BF)


def experts_pass(k, count, group, n2, cot, keep, weights_all, weights, grad, kept):
    rows, depth = n2.shape
    blocks, _, experts, ff, tile = weights.shape
    router_col = weights_all.shape[1] // LANES - 1
    const = lambda *shape: pl.BlockSpec(shape, lambda e: (0,) * len(shape))
    near = lambda e: jnp.minimum(e, experts - 1)
    far = lambda e: jnp.maximum(e - experts, 0)
    wide = pl.BlockSpec((1, rows, ff), lambda e: (k, 0, near(e)))
    part = pl.BlockSpec((rows, tile), lambda e: (0, far(e)))
    aliased = list(kept or ())
    grad = jnp.zeros((8, LANES), F32) if grad is None else grad
    return pl.pallas_call(
        functools.partial(expert_kernel, group, experts),
        grid=(experts + blocks,),
        in_specs=[
            const(rows, depth),
            const(rows, depth),
            pl.BlockSpec((1, rows, LANES), lambda e: (k, 0, 0)),
            pl.BlockSpec((depth, LANES), lambda e: (0, router_col)),
            pl.BlockSpec((tile, LANES), lambda e: (far(e), router_col)),
            pl.BlockSpec((blocks, 3, 1, ff, tile), lambda e: (0, 0, near(e), 0, 0)),
            pl.BlockSpec((1, 3, experts, ff, tile), lambda e: (far(e), 0, 0, 0, 0)),
            const(*grad.shape),
        ]
        + [pl.BlockSpec(memory_space=pl.ANY)] * len(aliased),
        out_specs=[wide, wide, wide, part, part, const(rows, LANES)],
        out_shape=[struct((count, rows, experts * ff), BF)] * 3
        + [struct((rows, depth), BF)] * 2
        + [struct((rows, LANES), BF if group == GROUPS - 1 else F32)],
        input_output_aliases={8 + i: i for i in range(len(aliased))},
        scratch_shapes=[pltpu.VMEM((rows, LANES), F32)] * 3
        + [pltpu.VMEM((rows, experts * ff), BF)] * 3
        + [pltpu.VMEM((3, ff, depth), BF), pltpu.VMEM((rows, LANES), BF)],
        compiler_params=params(1),
        cost_estimate=cost(
            6 * rows * depth * ff * experts,
            6 * experts * depth * ff * 2 + 4 * rows * depth * 2 + 3 * rows * experts * ff * 2,
            2 * rows * ff * experts,
        ),
        name=f"experts_{group}",
    )(n2, cot, keep, weights_all, weights_all, weights, weights, grad, *aliased)


def row_grad_kernel(count, plan, router, gain, *refs):
    ins = list(refs)
    lefts, rights = [], []
    for parts, tiles in plan:
        lefts.append([ins.pop(0) for _ in range(parts)])
        rights.append([ins.pop(0) for _ in tiles])
    dls = [ins.pop(0) for _ in range(count)] if router else []
    weight_ref = ins.pop(0) if gain else None
    out_ref, extra_ref, turned = ins.pop(0), ins.pop(0) if router or gain else None, ins.pop(0)
    i = pl.program_id(0)
    start = 0
    for (parts, tiles), left, right in zip(plan, lefts, rights):
        rows = left[0].shape[0]

        @pl.when(i == start)
        def _():
            for k in range(parts):
                turned[:, k * rows : (k + 1) * rows] = left[k][...].T
            if router and start == 0:
                total = None
                for k in range(count):
                    part = dot_nn(turned[:, k * rows : (k + 1) * rows], dls[k][...])
                    total = part if total is None else total + part
                extra_ref[...] = total
            if gain:
                extra_ref[...] = jnp.zeros_like(extra_ref)

        for ref, steps in zip(right, tiles):

            @pl.when(jnp.logical_and(i >= start, i < start + steps))
            def _():
                tile = out_ref.shape[1]
                full = dot_nn(turned[:, : parts * rows], ref[...].reshape(parts * rows, tile))
                out_ref[...] = full.astype(BF)
                if gain:
                    product = full * weight_ref[...].astype(F32)
                    for j in range(tile // LANES):
                        extra_ref[...] += product[:, j * LANES : (j + 1) * LANES]

            start += steps


def row_grads(pairs, tile, name, dls=(), weights=None):
    plan, args, specs, start, macs = [], [], [], 0, 0
    depth = pairs[0][0][0].shape[1]
    most = max(sum(part.shape[0] for part in left) for left, _ in pairs)

    def piece(array, first, steps):
        lead = array.shape[:-1]
        return pl.BlockSpec(
            lead + (tile,),
            lambda i: (0,) * len(lead) + (jnp.clip(i - first, 0, steps - 1),),
        )

    whole = pl.Buffered(1)
    for left, right in pairs:
        args += left
        specs += [pl.BlockSpec(p.shape, lambda i: (0, 0), pipeline_mode=whole) for p in left]
        tiles = []
        for array in right:
            steps = array.shape[-1] // tile
            args.append(array)
            specs.append(piece(array, start, steps))
            tiles.append(steps)
            start += steps
            macs += len(left) * left[0].shape[0] * depth * steps * tile
        plan.append((len(left), tuple(tiles)))
    out_specs = [pl.BlockSpec((depth, tile), lambda i: (0, i))]
    out_shape = [struct((depth, start * tile), BF)]
    if dls:
        args += dls
        specs += [pl.BlockSpec(d.shape, lambda i: (0, 0)) for d in dls]
    if weights is not None:
        args.append(weights)
        specs.append(pl.BlockSpec((depth, tile), lambda i: (0, i)))
    if dls or weights is not None:
        out_specs.append(pl.BlockSpec((depth, LANES), lambda i: (0, 0)))
        out_shape.append(struct((depth, LANES), F32))
    return pl.pallas_call(
        functools.partial(row_grad_kernel, len(dls), tuple(plan), bool(dls), weights is not None),
        grid=(start,),
        in_specs=specs,
        out_specs=out_specs,
        out_shape=out_shape,
        scratch_shapes=[pltpu.VMEM((depth, most), BF)],
        compiler_params=params(1),
        cost_estimate=cost(macs if 'experts' in name else macs // 16, 2 * depth * start * tile + 4 * most * depth),
        name=name,
    )(*args)


def per_device(
    tokens,
    lengths,
    routes,
    slot_order,
    attn_gain,
    query_gain,
    key_gain,
    query_weight,
    key_weight,
    value_weight,
    out_weight,
    moe_gain,
    router_weight,
    gate_weight,
    up_weight,
    down_weight,
    cotangent,
):
    per, seqs, depth = tokens.shape
    count = lax.axis_size("tp")
    me = lax.axis_index("tp")
    length = per * count
    rows = seqs * per
    head_width = query_gain.shape[0]
    local = query_weight.shape[1]
    scale = head_width ** (-0.5)

    first = jnp.concatenate(
        [
            query_weight,
            key_weight,
            value_weight,
            jnp.pad(router_weight, ((0, 0), (0, LANES - EXPERTS))),
        ],
        axis=1,
    )
    weights_all = lax.all_gather(first, "fsdp", axis=0, tiled=True)

    tok = jnp.transpose(tokens, (1, 0, 2)).reshape(rows, depth)
    tok_float = tok.astype(F32)
    n1_own = (tok_float * rms_scale(tok_float) * attn_gain).astype(BF)
    n1 = [n1_own, shift(n1_own, count, 1)]
    turned = jnp.stack(
        [jnp.swapaxes(gate_weight, 1, 2), jnp.swapaxes(up_weight, 1, 2), down_weight]
    )
    turned = after(turned, weights_all, n1[1])
    each = EXPERTS // GROUPS
    gather = lambda value: lax.all_gather(value, "fsdp", axis=0, tiled=False)
    moe_weights = [gather(turned[:, g * each : (g + 1) * each]) for g in range(GROUPS)]

    own_pos = me * per + jnp.arange(per, dtype=jnp.int32)
    valid_own = own_pos[None, :] < lengths[:, None]
    route_t = jnp.transpose(routes, (2, 1, 0)).reshape(TOP, rows)
    order_t = jnp.transpose(slot_order, (2, 1, 0)).reshape(TOP, rows)
    names = jnp.arange(EXPERTS, dtype=jnp.int32)[:, None]
    order_own = jnp.full((EXPERTS, rows), FAR, jnp.int32)
    for j in range(TOP):
        order_own = jnp.where(route_t[j][None, :] == names, order_t[j][None, :], order_own)
    order_own = jnp.where(valid_own.reshape(1, rows), order_own, FAR)
    owner = (me - jnp.arange(count, dtype=jnp.int32)) % count
    chunk_pos = owner[:, None] * per + jnp.arange(per, dtype=jnp.int32)[None, :]
    half = head_width // 2
    frequency = ROPE_BASE ** (-(jnp.arange(half, dtype=F32) * 2.0 / head_width))
    angles = chunk_pos.astype(F32)[:, :, None] * frequency
    cos_half, sin_half = jnp.cos(angles), jnp.sin(angles)
    cos = jnp.concatenate([cos_half, cos_half], axis=-1)
    sin = jnp.concatenate([-sin_half, sin_half], axis=-1)
    key_valid = (chunk_pos.reshape(1, length) < lengths[:, None]).astype(F32)
    key_valid = jnp.broadcast_to(key_valid[:, :, None], (seqs, length, LANES))

    gain_q, gain_k = query_gain[None, :], key_gain[None, :]
    kept, done = None, []
    for k in range(count):
        if k > 1:
            n1.append(shift(after(n1[-1], *done[: k - 2]), count, 1))
        kept = project(
            k, count, seqs, after(n1[k], *done[-1:]), weights_all, cos, sin, gain_q, gain_k, kept
        )
        done.append(kept[4])
    outs = ring_gather(after(out_weight, n1[-1]), count, -1)
    orders = ring_gather(after(order_own, n1[-1]), count)
    q_raw, k_raw, q, k_low, v = kept
    out_all = gather(after(jnp.concatenate(outs, axis=0), moe_weights[0], v))

    cot = jnp.transpose(cotangent, (1, 0, 2)).reshape(rows, depth)
    cot_own = jnp.where(valid_own.reshape(rows, 1), cot, jnp.zeros_like(cot))
    cots = [cot_own, shift(after(cot_own, n1[-1], outs[-1], orders[-1]), count, 1)]
    keep = keep_rows(after(jnp.stack(orders), v), length * seqs * TOP)

    ob, lse = attend(q, k_low, v, key_valid, scale)
    ob_rows = after(ob.reshape(count, rows, local), cots[1], keep)
    ob_parts = [ob_rows[0]] + [shift(ob_rows[s], count, -s) for s in range(1, count)]
    x1 = out_project(tok, ob_parts, out_all)
    n2_own = (x1 * rms_scale(x1) * moe_gain).astype(BF)
    n2 = [n2_own, shift(n2_own, count, 1)]
    cots.append(shift(after(cots[1], *ob_parts[1:]), count, 1))
    token = [n2_own]

    bufs = [None] * GROUPS
    ys = [[] for _ in range(count)]
    dns = [[] for _ in range(count)]
    grads = [None] * count

    def run(group, k):
        hp, da, du, y_k, dn_k, grads[k] = experts_pass(
            k, count, group, after(n2[k], *token), cots[k], keep, weights_all, moe_weights[group],
            grads[k], bufs[group],
        )
        bufs[group] = (hp, da, du)
        ys[k].append(y_k)
        dns[k].append(dn_k)
        token[0] = dn_k
        return dn_k

    def next_inputs(done):
        if len(n2) < count:
            n2.append(shift(after(n2[-1], done), count, 1))
        if len(cots) < count:
            cots.append(shift(after(cots[-1], done), count, 1))

    def both(parts):
        return plus(parts[0], *parts[1:]).astype(BF)

    ready = run(0, 0)
    next_inputs(ready)
    run(0, 1)
    ready = run(1, 0)
    next_inputs(ready)
    for k in range(2, count):
        run(0, k)
        if k < count - 1:
            next_inputs(run(1, k - 1))
    dn_run = shift(both(dns[1]), count, 1)
    token.append(dn_run)
    y_run = shift(after(both(ys[1]), dns[count - 1][0]), count, 1)
    ff = gate_weight.shape[2]
    hp, da, du = bufs[0]
    first_full = row_grads(
        [([after(n2[0], *token)] + n2[1:], [da, du]), (cots, [hp])], ff, "experts_first_grads"
    )[0]
    first_own = lax.psum_scatter(first_full, "fsdp", scatter_dimension=0, tiled=True)
    token = [first_full, y_run]
    run(1, count - 2)
    for k in range(2, count):
        dn_run = plus(dn_run, *dns[k]).astype(BF)
        token.append(dn_run)
        if k == count - 2:
            run(1, count - 1)
        dn_run = shift(dn_run, count, 1)
    hp, da, du = bufs[1]
    last_full, router_term = row_grads(
        [([after(n2[0], *token)] + n2[1:], [da, du])], ff, "experts_last_grads", grads
    )
    dn2 = plus(after(dn_run, last_full), *dns[0])

    moe_back, moe_gain_term = norm_back(dn2, x1, moe_gain)
    dx1 = moe_back + cot_own.astype(F32)
    db = dx1.astype(BF)
    dob = out_back(db, out_all, count)
    last_own = lax.psum_scatter(after(last_full, dob), "fsdp", scatter_dimension=0, tiled=True)
    dob = after(dob, first_own)
    dob_parts = [dob[0]] + [shift(dob[s], count, s) for s in range(1, count)]
    rest_full = row_grads(
        [(cots, [hp]), ([after(db, dob)], ob_parts)], ff, "rest_grads"
    )[0]
    d_ob = jnp.stack(dob_parts).reshape(count, seqs, per, local)
    d_ob = after(d_ob, rest_full)
    y_run = shift(after(plus(y_run, *ys[2]).astype(BF), d_ob), count, 1)

    dq, dk, dv, gains = attend_back(
        q, k_low, v, ob, d_ob, lse, key_valid, q_raw, k_raw, cos, sin, gain_q, gain_k, scale
    )
    part = input_back(1, after(dq, y_run), dk, dv, weights_all)
    rest_own = lax.psum_scatter(after(rest_full, part), "fsdp", scatter_dimension=0, tiled=True)
    dn1_run = shift(part, count, 1)
    qkv_full, attn_gain_wide = row_grads(
        [([after(n1[0], part)] + n1[1:], [a.reshape(count * rows, local) for a in (dq, dk, dv)])],
        min(256, local), "qkv_grads", weights=weights_all,
    )
    qkv_own = lax.psum_scatter(qkv_full, "fsdp", scatter_dimension=0, tiled=True)

    attn_gain_term = jnp.sum(attn_gain_wide, axis=1) / attn_gain
    packed = jnp.concatenate(
        [router_term[:, :EXPERTS].reshape(-1, LANES)]
        + [v.reshape(-1, LANES) for v in (attn_gain_term, moe_gain_term, gains[:2])],
        axis=0,
    )
    bits = [1 << b for b in range(count.bit_length() - 1)]
    across = lambda value, axis, bit: value + lax.ppermute(
        value, axis, [(i, i ^ bit) for i in range(lax.axis_size(axis))]
    )

    part = input_back(2, after(dq, qkv_full), dk, dv, weights_all)
    dn1_run = after(dn1_run, last_own)
    for k in range(2, count):
        dn1_run = plus(dn1_run, part).astype(BF)
        if k - 2 < len(bits):
            packed = across(after(packed, dn1_run), "tp", bits[k - 2])
        dn1_run = shift(dn1_run, count, 1)
        part = input_back((k + 1) % count, dq, dk, dv, weights_all)
    dn1 = plus(dn1_run, part)
    for k in range(3, count):
        y_run = shift(after(plus(y_run, *ys[k]).astype(BF), dn1_run), count, 1)
    for bit in bits[max(count - 2, 0) :]:
        packed = across(packed, "tp", bit)
    for b in range(lax.axis_size("fsdp").bit_length() - 1):
        packed = across(packed, "fsdp", 1 << b)

    layer_out = (x1 + plus(y_run, *ys[0])).astype(BF)

    qkv_sum = qkv_own.astype(F32)
    out_own = after(rest_own, dn1_run)[:, each * ff :]
    out_pieces = [out_own[:, s * local : (s + 1) * local] for s in range(count)]
    out_weight_grad = jnp.transpose(ring_scatter(out_pieces, -1))

    def expert_out(owns, axes):
        shaped = [own.reshape(own.shape[0], each, ff) for own in owns]
        return jnp.concatenate([jnp.transpose(v, axes) for v in shaped], axis=0).astype(F32)

    wide = each * ff
    gate_grad = expert_out((first_own[:, :wide], last_own[:, :wide]), (1, 0, 2))
    up_grad = expert_out((first_own[:, wide : 2 * wide], last_own[:, wide:]), (1, 0, 2))
    down_grad = expert_out((first_own[:, 2 * wide :], rest_own[:, :wide]), (1, 2, 0))

    attn_back = norm_back(dn1, tok_float, attn_gain)[0]
    tokens_grad = attn_back + dx1

    split = depth * EXPERTS // LANES
    across = depth // LANES
    small = (
        packed[split : split + across].reshape(depth),
        packed[split + 2 * across],
        packed[split + 2 * across + 1],
        packed[split + across : split + 2 * across].reshape(depth),
        packed[:split].reshape(depth, EXPERTS),
    )
    router_rows = depth // lax.axis_size("fsdp")
    router_grad = lax.dynamic_slice_in_dim(
        small[4], lax.axis_index("fsdp") * router_rows, router_rows, 0
    )

    def back_to_positions(value):
        return jnp.transpose(value.reshape(seqs, per, depth), (1, 0, 2))

    return (
        back_to_positions(layer_out),
        back_to_positions(tokens_grad),
        small[0],
        small[1],
        small[2],
        qkv_sum[:, :local],
        qkv_sum[:, local : 2 * local],
        qkv_sum[:, 2 * local :],
        out_weight_grad,
        small[3],
        router_grad,
        gate_grad,
        up_grad,
        down_grad,
    )


def solution(mesh):
    return jax.shard_map(
        per_device,
        mesh=mesh,
        in_specs=(
            P("tp", "fsdp", None),
            P("fsdp"),
            P("tp", "fsdp", None),
            P("tp", "fsdp", None),
            P(),
            P(),
            P(),
            P("fsdp", "tp"),
            P("fsdp", "tp"),
            P("fsdp", "tp"),
            P("tp", "fsdp"),
            P(),
            P("fsdp", None),
            P(None, "fsdp", "tp"),
            P(None, "fsdp", "tp"),
            P(None, "tp", "fsdp"),
            P("tp", "fsdp", None),
        ),
        out_specs=(
            P("tp", "fsdp", None),
            P("tp", "fsdp", None),
            P(),
            P(),
            P(),
            P("fsdp", "tp"),
            P("fsdp", "tp"),
            P("fsdp", "tp"),
            P("tp", "fsdp"),
            P(),
            P("fsdp", None),
            P(None, "fsdp", "tp"),
            P(None, "fsdp", "tp"),
            P(None, "tp", "fsdp"),
        ),
        check_vma=False,
    )
```

```python
import functools

import jax
import jax.numpy as jnp
from jax import lax
from jax.experimental import pallas as pl
from jax.experimental.pallas import tpu as pltpu
from jax.sharding import PartitionSpec as P

EXPERTS = 16
TOP = 8
CAP = 1280
LANES = 128

EPS = 1e-06
ROPE_BASE = 10000.0
NEG_FILL = -1e30
FAR = 1 << 20
BF = jnp.bfloat16
F32 = jnp.float32
VMEM_BYTES = 58 * 1024 * 1024
GROUPS = 2


def dot_nn(a, b):
    return lax.dot_general(a, b, (((1,), (0,)), ((), ())), preferred_element_type=F32)


def dot_nt(a, b):
    return lax.dot_general(a, b, (((1,), (1,)), ((), ())), preferred_element_type=F32)


def dot_tn(a, b):
    return lax.dot_general(a, b, (((0,), (0,)), ((), ())), preferred_element_type=F32)


def params(steps):
    return pltpu.CompilerParams(
        dimension_semantics=("arbitrary",) * steps, vmem_limit_bytes=VMEM_BYTES
    )


def cost(macs, nbytes, exps=0):
    return pl.CostEstimate(flops=32 * macs, bytes_accessed=nbytes, transcendentals=exps)


def struct(shape, dtype):
    return jax.ShapeDtypeStruct(shape, dtype)


def rms_scale(values):
    return lax.rsqrt(jnp.mean(values * values, axis=-1, keepdims=True) + EPS)


def norm_back(grad_in, raw_values, gain_values):
    scale_rows = rms_scale(raw_values)
    normed = raw_values * scale_rows
    scaled = grad_in * gain_values
    grad_raw = scale_rows * (scaled - normed * jnp.mean(scaled * normed, axis=-1, keepdims=True))
    grad_gain = jnp.sum(grad_in * normed, axis=tuple(range(grad_in.ndim - 1)))
    return (grad_raw, grad_gain)


def shift(value, count, step):
    return lax.ppermute(value, "tp", [(i, (i + step) % count) for i in range(count)])


def after(value, *done):
    return lax.optimization_barrier((value,) + done)[0]


def exchange(parts, step):
    return [parts[0]] + [shift(parts[s], len(parts), s * step) for s in range(1, len(parts))]


def plus(arrived, *parts):
    total = arrived.astype(F32)
    for part in parts:
        total = total + part.astype(F32)
    return total


def keep_kernel(bits, order_ref, keep_ref):
    count, experts, rows = order_ref.shape

    def below(limit):
        found = jnp.zeros((experts, 1), jnp.int32)
        for k in range(count):
            found = found + jnp.sum(
                (order_ref[k] < limit).astype(jnp.int32), axis=1, keepdims=True
            )
        return found

    last = jnp.zeros((experts, 1), jnp.int32)
    for bit in range(bits - 1, -1, -1):
        trial = last + (1 << bit)
        last = jnp.where(below(trial) < CAP, trial, last)
    for k in range(count):
        keep = (order_ref[k] <= last).astype(F32)
        wide = jnp.concatenate([keep, jnp.zeros((LANES - experts, rows), F32)], axis=0)
        keep_ref[k] = wide.T


def keep_rows(order_all, pair_count):
    count, experts, rows = order_all.shape
    return pl.pallas_call(
        functools.partial(keep_kernel, pair_count.bit_length() + 1),
        out_shape=struct((count, rows, LANES), F32),
        compiler_params=pltpu.CompilerParams(vmem_limit_bytes=VMEM_BYTES),
        cost_estimate=cost(16 * count * experts * rows, count * rows * LANES * 4),
        name="keep_rows",
    )(order_all)


def qkv_kernel(seqs, x_ref, wq_ref, wk_ref, wv_ref, cos_ref, sin_ref, gq_ref, gk_ref, *rest):
    qr_ref, kr_ref, q_ref, k_ref, v_ref = rest[-5:]
    rows = x_ref.shape[0] // seqs
    width = wq_ref.shape[1]
    heads = width // LANES
    x = x_ref[...]
    for w_ref, raw_ref, low_ref, gain_ref in (
        (wq_ref, qr_ref, q_ref, gq_ref),
        (wk_ref, kr_ref, k_ref, gk_ref),
    ):
        raw = dot_nn(x, w_ref[...])
        for s in range(seqs):
            for h in range(heads):
                part = raw[s * rows : (s + 1) * rows, h * LANES : (h + 1) * LANES]
                raw_ref[0, s, :, h * LANES : (h + 1) * LANES] = part
                normed = part * rms_scale(part) * gain_ref[...]
                turned = normed * cos_ref[0] + pltpu.roll(normed, LANES // 2, 1) * sin_ref[0]
                low_ref[0, s, :, h * LANES : (h + 1) * LANES] = turned.astype(BF)
    value = dot_nn(x, wv_ref[...]).astype(BF)
    for s in range(seqs):
        v_ref[0, s] = value[s * rows : (s + 1) * rows]


def project(k, count, seqs, x, weights, cos, sin, gain_q, gain_k, kept):
    rows, depth = x.shape
    local = (weights.shape[1] - LANES) // 3
    group = min(256, local)
    groups = local // group
    per = rows // seqs
    const = lambda *shape: pl.BlockSpec(shape, lambda g: (0,) * len(shape))
    table = pl.BlockSpec((1, per, LANES), lambda g: (k, 0, 0))
    out = pl.BlockSpec((1, seqs, per, group), lambda g: (k, 0, 0, g))
    shapes = [struct((count, seqs, per, local), d) for d in (F32, F32, BF, BF, BF)]
    aliased = list(kept or ())
    return pl.pallas_call(
        functools.partial(qkv_kernel, seqs),
        grid=(groups,),
        in_specs=[
            const(rows, depth),
            pl.BlockSpec((depth, group), lambda g: (0, g)),
            pl.BlockSpec((depth, group), lambda g: (0, groups + g)),
            pl.BlockSpec((depth, group), lambda g: (0, 2 * groups + g)),
            table,
            table,
            const(1, LANES),
            const(1, LANES),
        ]
        + [pl.BlockSpec(memory_space=pl.ANY)] * len(aliased),
        out_specs=[out] * 5,
        out_shape=shapes,
        input_output_aliases={8 + i: i for i in range(len(aliased))},
        compiler_params=params(1),
        cost_estimate=cost(rows * depth * local * 3 // 16, rows * depth * 2 + depth * local * 6),
        name="project",
    )(x, weights, weights, weights, cos, sin, gain_q, gain_k, *aliased)


def attend_kernel(scale, q_ref, k_ref, v_ref, valid_ref, o_ref, lse_ref):
    count, _, rows, width = q_ref.shape
    length = count * rows
    keys = k_ref[...].reshape(length, width)
    values_t = v_ref[...].reshape(length, width).astype(F32).T.astype(BF)
    valid = valid_ref[0][:, :1] > 0
    for i in range(count):
        scores = dot_nt(keys, q_ref[i, 0]) * scale
        weights = jnp.exp(jnp.where(valid, scores, NEG_FILL))
        total = jnp.sum(weights, axis=0, keepdims=True)
        out_t = dot_nn(values_t, weights.astype(BF)) / total
        o_ref[i, 0] = out_t.T.astype(BF)
        lse_ref[0, i : i + 1, :] = jnp.log(total)


def attend(q, k, v, valid, scale):
    count, seqs, rows, local = q.shape
    heads = local // LANES
    head = pl.BlockSpec((count, 1, rows, LANES), lambda s, h: (0, s, 0, h))
    return pl.pallas_call(
        functools.partial(attend_kernel, scale),
        grid=(seqs, heads),
        in_specs=[head, head, head, pl.BlockSpec((1, count * rows, LANES), lambda s, h: (s, 0, 0))],
        out_specs=[head, pl.BlockSpec((1, count, rows), lambda s, h: (s * heads + h, 0, 0))],
        out_shape=[struct(q.shape, BF), struct((seqs * heads, count, rows), F32)],
        compiler_params=params(2),
        cost_estimate=cost(
            2 * seqs * local * (count * rows) ** 2,
            4 * count * seqs * rows * local * 2,
            seqs * heads * (count * rows) ** 2,
        ),
        name="attend",
    )(q, k, v, valid)


def attend_back_kernel(scale, *refs):
    q_ref, k_ref, v_ref, o_ref, do_ref, lse_ref, valid_ref = refs[:7]
    qr_ref, kr_ref, cos_ref, sin_ref, gq_ref, gk_ref = refs[7:13]
    dq_ref, dk_ref, dv_ref, gains_ref = refs[13:17]
    dk_acc, dv_acc = refs[17:]
    count, _, rows, width = q_ref.shape
    length = count * rows
    first = jnp.logical_and(pl.program_id(0) == 0, pl.program_id(1) == 0)

    @pl.when(first)
    def _():
        gains_ref[...] = jnp.zeros_like(gains_ref)

    keys = k_ref[...].reshape(length, width)
    keys_t = keys.astype(F32).T.astype(BF)
    values = v_ref[...].reshape(length, width)
    valid = valid_ref[0][:, :1] > 0
    ones = jnp.ones((8, width), F32)

    def back(grad, raw, cos, sin, gain):
        turned = grad * cos - pltpu.roll(grad, LANES // 2, 1) * sin
        scale_rows = rms_scale(raw)
        normed = raw * scale_rows
        scaled = turned * gain
        mean = jnp.mean(scaled * normed, axis=-1, keepdims=True)
        return scale_rows * (scaled - normed * mean), jnp.sum(
            turned * normed, axis=0, keepdims=True
        )

    gain_q = jnp.zeros((1, width), F32)
    gain_k = jnp.zeros((1, width), F32)
    for i in range(count):
        query = q_ref[i, 0]
        grad = do_ref[i, 0]
        scores = dot_nt(keys, query) * scale
        weights = jnp.exp(jnp.where(valid, scores, NEG_FILL) - lse_ref[0, i : i + 1, :])
        delta = jnp.sum(
            (grad.astype(F32) * o_ref[i, 0].astype(F32)).T, axis=0, keepdims=True
        )
        d_weights = dot_nt(values, grad)
        d_scores = (weights * (d_weights - delta)).astype(BF)
        dv_part = dot_nn(weights.astype(BF), grad)
        dk_part = dot_nn(d_scores, query)
        if i == 0:
            dv_acc[...] = dv_part
            dk_acc[...] = dk_part
        else:
            dv_acc[...] += dv_part
            dk_acc[...] += dk_part
        dq = (dot_nn(keys_t, d_scores) * scale).T
        d_raw, d_gain = back(dq, qr_ref[i, 0], cos_ref[i], sin_ref[i], gq_ref[...])
        gain_q = gain_q + d_gain
        dq_ref[i, 0] = d_raw.astype(BF)
    for i in range(count):
        dv_ref[i, 0] = dv_acc[i * rows : (i + 1) * rows].astype(BF)
        dk = dk_acc[i * rows : (i + 1) * rows] * scale
        d_raw, d_gain = back(dk, kr_ref[i, 0], cos_ref[i], sin_ref[i], gk_ref[...])
        gain_k = gain_k + d_gain
        dk_ref[i, 0] = d_raw.astype(BF)
    gains_ref[0:1, :] += gain_q
    gains_ref[1:2, :] += gain_k


def attend_back(q, k, v, o, do, lse, valid, q_raw, k_raw, cos, sin, gain_q, gain_k, scale):
    count, seqs, rows, local = q.shape
    heads = local // LANES
    head = pl.BlockSpec((count, 1, rows, LANES), lambda s, h: (0, s, 0, h))
    const = lambda *shape: pl.BlockSpec(shape, lambda s, h: (0,) * len(shape))
    return pl.pallas_call(
        functools.partial(attend_back_kernel, scale),
        grid=(seqs, heads),
        in_specs=[
            head,
            head,
            head,
            head,
            head,
            pl.BlockSpec((1, count, rows), lambda s, h: (s * heads + h, 0, 0)),
            pl.BlockSpec((1, count * rows, LANES), lambda s, h: (s, 0, 0)),
            head,
            head,
            const(count, rows, LANES),
            const(count, rows, LANES),
            const(1, LANES),
            const(1, LANES),
        ],
        out_specs=[head, head, head, const(8, LANES)],
        out_shape=[struct(q.shape, BF)] * 3 + [struct((8, LANES), F32)],
        scratch_shapes=[pltpu.VMEM((count * rows, LANES), F32)] * 2,
        compiler_params=params(2),
        cost_estimate=cost(
            5 * seqs * local * (count * rows) ** 2,
            12 * count * seqs * rows * local * 2,
            seqs * heads * (count * rows) ** 2,
        ),
        name="attend_back",
    )(q, k, v, o, do, lse, valid, q_raw, k_raw, cos, sin, gain_q, gain_k)


def input_back_kernel(dq_ref, dk_ref, dv_ref, wq_ref, wk_ref, wv_ref, out_ref):
    total = None
    for d_ref, w_ref in ((dq_ref, wq_ref), (dk_ref, wk_ref), (dv_ref, wv_ref)):
        grad = d_ref[0].reshape(out_ref.shape[0], w_ref.shape[1])
        part = dot_nt(grad, w_ref[...])
        total = part if total is None else total + part
    out_ref[...] = total.astype(BF)


def input_back(k, dq, dk, dv, weights):
    _, seqs, per, local = dq.shape
    depth = weights.shape[0]
    rows = seqs * per
    tile = min(512, depth)
    grad = pl.BlockSpec((1, seqs, per, local), lambda t: (k, 0, 0, 0))
    return pl.pallas_call(
        input_back_kernel,
        grid=(depth // tile,),
        in_specs=[grad] * 3
        + [pl.BlockSpec((tile, local), lambda t, j=j: (t, j)) for j in range(3)],
        out_specs=pl.BlockSpec((rows, tile), lambda t: (0, t)),
        out_shape=struct((rows, depth), BF),
        compiler_params=params(1),
        cost_estimate=cost(rows * depth * local * 3 // 16, rows * depth * 2 + depth * local * 6),
        name="input_back",
    )(dq, dk, dv, weights, weights, weights)


def out_kernel(count, tok_ref, *refs):
    ob_refs = refs[:count]
    w_ref, x1_ref = refs[count:]
    local = ob_refs[0].shape[1]
    total = tok_ref[...].astype(F32)
    for s in range(count):
        total = total + dot_nn(ob_refs[s][...], w_ref[0, s * local : (s + 1) * local, :])
    x1_ref[...] = total


def out_project(tok, parts, weights):
    rows, depth = tok.shape
    blocks, full, tile = weights.shape
    count = len(parts)
    return pl.pallas_call(
        functools.partial(out_kernel, count),
        grid=(blocks,),
        in_specs=[pl.BlockSpec((rows, tile), lambda j: (0, j))]
        + [pl.BlockSpec(parts[0].shape, lambda j: (0, 0))] * count
        + [pl.BlockSpec((1, full, tile), lambda j: (j, 0, 0))],
        out_specs=pl.BlockSpec((rows, tile), lambda j: (0, j)),
        out_shape=struct((rows, depth), F32),
        compiler_params=params(1),
        cost_estimate=cost(rows * depth * full, rows * depth * 8 + full * depth * 2),
        name="out_project",
    )(tok, *parts, weights)


def out_back_kernel(db_ref, w_ref, out_ref):
    blocks, _, tile = w_ref.shape
    total = None
    for j in range(blocks):
        part = dot_nt(db_ref[:, j * tile : (j + 1) * tile], w_ref[j])
        total = part if total is None else total + part
    out_ref[0] = total.astype(BF)


def out_back(db, weights, count):
    rows, depth = db.shape
    blocks, full, tile = weights.shape
    local = full // count
    return pl.pallas_call(
        out_back_kernel,
        grid=(count,),
        in_specs=[
            pl.BlockSpec((rows, depth), lambda s: (0, 0)),
            pl.BlockSpec((blocks, local, tile), lambda s: (0, s, 0)),
        ],
        out_specs=pl.BlockSpec((1, rows, local), lambda s: (s, 0, 0)),
        out_shape=struct((count, rows, local), BF),
        compiler_params=params(1),
        cost_estimate=cost(rows * depth * full, rows * depth * 2 + full * depth * 2),
        name="out_back",
    )(db, weights)


def expert_kernel(group, experts, n2_ref, c_ref, keep_ref, router_ref, tile_ref, w_ref, *rest):
    last = group == GROUPS - 1
    wt_ref, grad_in, y_in, dn_in = rest[:4]
    hp_ref, da_ref, du_ref, y_ref, dn_ref, grad_out = rest[-14:-8]
    probs, gates, grads, hp_all, da_all, du_all, full, low = rest[-8:]
    e = pl.program_id(0)
    blocks, _, _, ff, tile = w_ref.shape
    rows = n2_ref.shape[0]
    lane = lax.broadcasted_iota(jnp.int32, (rows, LANES), 1)

    @pl.when(e == 0)
    def _():
        logits = jnp.where(lane < EXPERTS, dot_nn(n2_ref[...], router_ref[...]), NEG_FILL)
        raised = jnp.exp(logits - jnp.max(logits, axis=-1, keepdims=True))
        soft = raised / jnp.sum(raised, axis=-1, keepdims=True)
        probs[...] = soft
        gates[...] = soft * keep_ref[0]
        grads[...] = jnp.zeros_like(grads) if group == 0 else grad_in[...]

    @pl.when(e < experts)
    def _():
        for t in range(3):
            for j in range(blocks):
                full[t, :, j * tile : (j + 1) * tile] = w_ref[j, t, 0]
        here = lane == e + group * experts
        gate = jnp.sum(jnp.where(here, gates[...], 0.0), axis=-1, keepdims=True)
        x = n2_ref[...]
        pre = dot_nt(x, full[0])
        up = dot_nt(x, full[1])
        back = dot_nt(c_ref[...], full[2])
        sig = 1.0 / (1.0 + jnp.exp(-pre))
        act = pre * sig
        hid = act * up
        hp = (hid * gate).astype(BF)
        column = jnp.sum(back * hid, axis=-1, keepdims=True)
        grads[...] += jnp.where(here, column * keep_ref[0], 0.0)
        dh = back * gate
        du = (dh * act).astype(BF)
        da = (dh * up * (sig + act * (1.0 - sig))).astype(BF)
        hp_ref[0] = hp
        da_ref[0] = da
        du_ref[0] = du
        place = pl.ds(pl.multiple_of(e * ff, ff), ff)
        hp_all[:, place] = hp
        da_all[:, place] = da
        du_all[:, place] = du

    @pl.when(e == experts - 1)
    def _():
        if last:
            soft = probs[...]
            gd = grads[...]
            dl = (soft * (gd - jnp.sum(soft * gd, axis=-1, keepdims=True))).astype(BF)
            grad_out[...] = dl
            low[...] = dl
        else:
            grad_out[...] = grads[...]

    @pl.when(e >= experts)
    def _():
        wide = experts * ff
        y = dot_nn(hp_all[...], wt_ref[0, 2].reshape(wide, tile))
        total = dot_nn(da_all[...], wt_ref[0, 0].reshape(wide, tile))
        total = total + dot_nn(du_all[...], wt_ref[0, 1].reshape(wide, tile))
        if last:
            total = total + dot_nt(low[...], tile_ref[...])
        if group > 0:
            y = y + y_in[...].astype(F32)
            total = total + dn_in[...].astype(F32)
        y_ref[...] = y.astype(BF)
        dn_ref[...] = total.astype(BF)


def experts_pass(k, count, group, n2, cot, keep, weights_all, weights, before, kept):
    rows, depth = n2.shape
    blocks, _, experts, ff, tile = weights.shape
    router_col = weights_all.shape[1] // LANES - 1
    const = lambda *shape: pl.BlockSpec(shape, lambda e: (0,) * len(shape))
    near = lambda e: jnp.minimum(e, experts - 1)
    far = lambda e: jnp.maximum(e - experts, 0)
    wide = pl.BlockSpec((1, rows, ff), lambda e: (k, 0, near(e)))
    part = pl.BlockSpec((rows, tile), lambda e: (0, far(e)))
    aliased = list(kept or ())
    grad, *sums = before or (jnp.zeros((8, LANES), F32),)
    return pl.pallas_call(
        functools.partial(expert_kernel, group, experts),
        grid=(experts + blocks,),
        in_specs=[
            const(rows, depth),
            const(rows, depth),
            pl.BlockSpec((1, rows, LANES), lambda e: (k, 0, 0)),
            pl.BlockSpec((depth, LANES), lambda e: (0, router_col)),
            pl.BlockSpec((tile, LANES), lambda e: (far(e), router_col)),
            pl.BlockSpec((blocks, 3, 1, ff, tile), lambda e: (0, 0, near(e), 0, 0)),
            pl.BlockSpec((1, 3, experts, ff, tile), lambda e: (far(e), 0, 0, 0, 0)),
            const(*grad.shape),
        ]
        + [part] * len(sums)
        + [pl.BlockSpec(memory_space=pl.ANY)] * len(aliased),
        out_specs=[wide, wide, wide, part, part, const(rows, LANES)],
        out_shape=[struct((count, rows, experts * ff), BF)] * 3
        + [struct((rows, depth), BF)] * 2
        + [struct((rows, LANES), BF if group == GROUPS - 1 else F32)],
        input_output_aliases={8 + len(sums) + i: i for i in range(len(aliased))},
        scratch_shapes=[pltpu.VMEM((rows, LANES), F32)] * 3
        + [pltpu.VMEM((rows, experts * ff), BF)] * 3
        + [pltpu.VMEM((3, ff, depth), BF), pltpu.VMEM((rows, LANES), BF)],
        compiler_params=params(1),
        cost_estimate=cost(
            6 * rows * depth * ff * experts,
            6 * experts * depth * ff * 2 + 4 * rows * depth * 2 + 3 * rows * experts * ff * 2,
            2 * rows * ff * experts,
        ),
        name=f"experts_{group}",
    )(n2, cot, keep, weights_all, weights_all, weights, weights, grad, *sums, *aliased)


def row_grad_kernel(count, plan, router, gain, *refs):
    ins = list(refs)
    lefts, rights = [], []
    for parts, tiles in plan:
        lefts.append([ins.pop(0) for _ in range(parts)])
        rights.append([ins.pop(0) for _ in tiles])
    dls = [ins.pop(0) for _ in range(count)] if router else []
    weight_ref = ins.pop(0) if gain else None
    out_ref, extra_ref, turned = ins.pop(0), ins.pop(0) if router or gain else None, ins.pop(0)
    i = pl.program_id(0)
    start = 0
    for (parts, tiles), left, right in zip(plan, lefts, rights):
        rows = left[0].shape[0]

        @pl.when(i == start)
        def _():
            for k in range(parts):
                turned[:, k * rows : (k + 1) * rows] = left[k][...].T
            if router and start == 0:
                total = None
                for k in range(count):
                    part = dot_nn(turned[:, k * rows : (k + 1) * rows], dls[k][...])
                    total = part if total is None else total + part
                extra_ref[...] = total
            if gain:
                extra_ref[...] = jnp.zeros_like(extra_ref)

        for ref, steps in zip(right, tiles):

            @pl.when(jnp.logical_and(i >= start, i < start + steps))
            def _():
                tile = out_ref.shape[1]
                full = dot_nn(turned[:, : parts * rows], ref[...].reshape(parts * rows, tile))
                out_ref[...] = full.astype(BF)
                if gain:
                    product = full * weight_ref[...].astype(F32)
                    for j in range(tile // LANES):
                        extra_ref[...] += product[:, j * LANES : (j + 1) * LANES]

            start += steps


def row_grads(pairs, tile, name, dls=(), weights=None):
    plan, args, specs, start, macs = [], [], [], 0, 0
    depth = pairs[0][0][0].shape[1]
    most = max(sum(part.shape[0] for part in left) for left, _ in pairs)

    def piece(array, first, steps):
        lead = array.shape[:-1]
        return pl.BlockSpec(
            lead + (tile,),
            lambda i: (0,) * len(lead) + (jnp.clip(i - first, 0, steps - 1),),
        )

    whole = pl.Buffered(1)
    for left, right in pairs:
        args += left
        specs += [pl.BlockSpec(p.shape, lambda i: (0, 0), pipeline_mode=whole) for p in left]
        tiles = []
        for array in right:
            steps = array.shape[-1] // tile
            args.append(array)
            specs.append(piece(array, start, steps))
            tiles.append(steps)
            start += steps
            macs += len(left) * left[0].shape[0] * depth * steps * tile
        plan.append((len(left), tuple(tiles)))
    out_specs = [pl.BlockSpec((depth, tile), lambda i: (0, i))]
    out_shape = [struct((depth, start * tile), BF)]
    if dls:
        args += dls
        specs += [pl.BlockSpec(d.shape, lambda i: (0, 0)) for d in dls]
    if weights is not None:
        args.append(weights)
        specs.append(pl.BlockSpec((depth, tile), lambda i: (0, i)))
    if dls or weights is not None:
        out_specs.append(pl.BlockSpec((depth, LANES), lambda i: (0, 0)))
        out_shape.append(struct((depth, LANES), F32))
    return pl.pallas_call(
        functools.partial(row_grad_kernel, len(dls), tuple(plan), bool(dls), weights is not None),
        grid=(start,),
        in_specs=specs,
        out_specs=out_specs,
        out_shape=out_shape,
        scratch_shapes=[pltpu.VMEM((depth, most), BF)],
        compiler_params=params(1),
        cost_estimate=cost(macs if 'experts' in name else macs // 16, 2 * depth * start * tile + 4 * most * depth),
        name=name,
    )(*args)


def per_device(
    tokens,
    lengths,
    routes,
    slot_order,
    attn_gain,
    query_gain,
    key_gain,
    query_weight,
    key_weight,
    value_weight,
    out_weight,
    moe_gain,
    router_weight,
    gate_weight,
    up_weight,
    down_weight,
    cotangent,
):
    per, seqs, depth = tokens.shape
    count = lax.axis_size("tp")
    me = lax.axis_index("tp")
    length = per * count
    rows = seqs * per
    head_width = query_gain.shape[0]
    local = query_weight.shape[1]
    scale = head_width ** (-0.5)

    first = jnp.concatenate(
        [
            query_weight,
            key_weight,
            value_weight,
            jnp.pad(router_weight, ((0, 0), (0, LANES - EXPERTS))),
        ],
        axis=1,
    )
    weights_all = lax.all_gather(first, "fsdp", axis=0, tiled=True)

    tok = jnp.transpose(tokens, (1, 0, 2)).reshape(rows, depth)
    tok_float = tok.astype(F32)
    n1_own = (tok_float * rms_scale(tok_float) * attn_gain).astype(BF)
    outs = exchange([after(out_weight, n1_own)] * count, -1)
    n1 = [n1_own, shift(after(n1_own, *outs[1:]), count, 1)]
    own_pos = me * per + jnp.arange(per, dtype=jnp.int32)
    valid_own = own_pos[None, :] < lengths[:, None]
    route_t = jnp.transpose(routes, (2, 1, 0)).reshape(TOP, rows)
    order_t = jnp.transpose(slot_order, (2, 1, 0)).reshape(TOP, rows)
    names = jnp.arange(EXPERTS, dtype=jnp.int32)[:, None]
    order_own = jnp.full((EXPERTS, rows), FAR, jnp.int32)
    for j in range(TOP):
        order_own = jnp.where(route_t[j][None, :] == names, order_t[j][None, :], order_own)
    order_own = jnp.where(valid_own.reshape(1, rows), order_own, FAR)
    orders = exchange([after(order_own, n1[1])] * count, 1)

    each = EXPERTS // GROUPS
    gather = lambda value: lax.all_gather(value, "fsdp", axis=0, tiled=False)

    def group_weights(g):
        part = slice(g * each, (g + 1) * each)
        stacked = jnp.concatenate(
            [
                jnp.swapaxes(gate_weight[part], 1, 2),
                jnp.swapaxes(up_weight[part], 1, 2),
                down_weight[part],
            ]
        )
        stacked = after(stacked, weights_all, n1[1])
        return gather(stacked.reshape((3, each) + stacked.shape[1:]))

    out_all = gather(jnp.concatenate(outs, axis=0))
    moe_weights = [group_weights(g) for g in range(GROUPS)]
    owner = (me - jnp.arange(count, dtype=jnp.int32)) % count
    chunk_pos = owner[:, None] * per + jnp.arange(per, dtype=jnp.int32)[None, :]
    half = head_width // 2
    frequency = ROPE_BASE ** (-(jnp.arange(half, dtype=F32) * 2.0 / head_width))
    angles = chunk_pos.astype(F32)[:, :, None] * frequency
    cos_half, sin_half = jnp.cos(angles), jnp.sin(angles)
    cos = jnp.concatenate([cos_half, cos_half], axis=-1)
    sin = jnp.concatenate([-sin_half, sin_half], axis=-1)
    key_valid = (chunk_pos.reshape(1, length) < lengths[:, None]).astype(F32)
    key_valid = jnp.broadcast_to(key_valid[:, :, None], (seqs, length, LANES))

    gain_q, gain_k = query_gain[None, :], key_gain[None, :]
    kept, done = None, []
    for k in range(count):
        if k > 1:
            n1.append(shift(after(n1[-1], *(done[: k - 1] if k > 2 else ())), count, 1))
        kept = project(
            k, count, seqs, after(n1[k], *done[-1:]), weights_all, cos, sin, gain_q, gain_k, kept
        )
        done.append(kept[4])
    q_raw, k_raw, q, k_low, v = kept
    keep = keep_rows(after(jnp.stack(orders), done[1]), length * seqs * TOP)

    cot = jnp.transpose(cotangent, (1, 0, 2)).reshape(rows, depth)
    cot_own = jnp.where(valid_own.reshape(rows, 1), cot, jnp.zeros_like(cot))
    cots = [cot_own, shift(after(cot_own, n1[-1], done[count - 2]), count, 1)]

    ob, lse = attend(q, k_low, v, key_valid, scale)
    ob_rows = after(ob.reshape(count, rows, local), cots[1])
    ob_parts = exchange(ob_rows, -1)
    x1 = out_project(tok, ob_parts, out_all)
    n2_own = (x1 * rms_scale(x1) * moe_gain).astype(BF)
    n2 = [n2_own, shift(n2_own, count, 1)]
    token = [n2_own]

    bufs = [None] * GROUPS
    ys, dns, grads = [None] * count, [None] * count, [None] * count

    def run(group, k):
        before = (grads[k], ys[k], dns[k]) if group else None
        hp, da, du, ys[k], dns[k], grads[k] = experts_pass(
            k, count, group, after(n2[k], *token), cots[k], keep, weights_all, moe_weights[group],
            before, bufs[group],
        )
        bufs[group] = (hp, da, du)
        token[0] = dns[k]
        return dns[k]

    def next_inputs(done):
        if len(n2) < count:
            n2.append(shift(after(n2[-1], done), count, 1))
        if len(cots) < count:
            cots.append(shift(after(cots[-1], done), count, 1))

    ready = run(0, 0)
    next_inputs(ready)
    run(0, 1)
    ready = run(1, 0)
    next_inputs(ready)
    for k in range(2, count):
        run(0, k)
        if k < count - 1:
            next_inputs(run(1, k - 1))
    dn_run = shift(dns[1], count, 1)
    token.append(dn_run)
    y_run = shift(after(ys[1], dns[count - 1]), count, 1)
    ff = gate_weight.shape[2]
    hp, da, du = bufs[0]
    first_full = row_grads(
        [([after(n2[0], *token)] + n2[1:], [da, du]), (cots, [hp])], ff, "experts_first_grads"
    )[0]
    first_own = lax.psum_scatter(first_full, "fsdp", scatter_dimension=0, tiled=True)
    token = [first_full, y_run]
    run(1, count - 2)
    for k in range(2, count):
        dn_run = plus(dn_run, dns[k]).astype(BF)
        token.append(dn_run)
        if k == count - 2:
            run(1, count - 1)
        dn_run = shift(dn_run, count, 1)
    hp, da, du = bufs[1]
    last_full, router_term = row_grads(
        [([after(n2[0], *token)] + n2[1:], [da, du])], ff, "experts_last_grads", grads
    )
    dn2 = plus(after(dn_run, last_full), dns[0])


    moe_back, moe_gain_term = norm_back(dn2, x1, moe_gain)
    dx1 = moe_back + cot_own.astype(F32)
    db = dx1.astype(BF)
    dob = out_back(db, out_all, count)
    last_own = lax.psum_scatter(after(last_full, dob), "fsdp", scatter_dimension=0, tiled=True)
    dob = after(dob, first_own)
    dob_parts = exchange(dob, 1)
    rest_full = row_grads(
        [(cots, [hp]), ([after(db, dob)], ob_parts)], ff, "rest_grads"
    )[0]
    d_ob = jnp.stack(dob_parts).reshape(count, seqs, per, local)
    y_sum = plus(after(y_run, dob), ys[2]).astype(BF)
    d_ob = after(d_ob, rest_full, y_sum)
    y_run = shift(after(y_sum, d_ob), count, 1)
    for k in range(3, count - 1):
        y_run = shift(plus(y_run, ys[k]).astype(BF), count, 1)

    dq, dk, dv, gains = attend_back(
        q, k_low, v, ob, d_ob, lse, key_valid, q_raw, k_raw, cos, sin, gain_q, gain_k, scale
    )
    part = input_back(1, after(dq, y_run), dk, dv, weights_all)
    rest_own = lax.psum_scatter(after(rest_full, d_ob), "fsdp", scatter_dimension=0, tiled=True)
    dn1_run = shift(part, count, 1)
    qkv_full, attn_gain_wide = row_grads(
        [([after(n1[0], part)] + n1[1:], [a.reshape(count * rows, local) for a in (dq, dk, dv)])],
        min(256, local), "qkv_grads", weights=weights_all,
    )
    qkv_own = lax.psum_scatter(qkv_full, "fsdp", scatter_dimension=0, tiled=True)

    attn_gain_term = jnp.sum(attn_gain_wide, axis=1) / attn_gain
    packed = jnp.concatenate(
        [router_term[:, :EXPERTS].reshape(-1, LANES)]
        + [v.reshape(-1, LANES) for v in (attn_gain_term, moe_gain_term, gains[:2])],
        axis=0,
    )
    bits = [1 << b for b in range(count.bit_length() - 1)]
    across = lambda value, axis, bit: value + lax.ppermute(
        value, axis, [(i, i ^ bit) for i in range(lax.axis_size(axis))]
    )

    part = input_back(2, after(dq, qkv_full), dk, dv, weights_all)
    dn1_run = after(dn1_run, last_own)
    for k in range(2, count):
        dn1_run = plus(dn1_run, part).astype(BF)
        if k - 2 < len(bits):
            packed = across(after(packed, dn1_run), "tp", bits[k - 2])
        dn1_run = shift(dn1_run, count, 1)
        part = input_back((k + 1) % count, dq, dk, dv, weights_all)
    dn1 = plus(dn1_run, part)
    for bit in bits[max(count - 2, 0) :]:
        packed = across(packed, "tp", bit)
    qkv_sum = qkv_own.astype(F32)
    out_own = rest_own[:, each * ff :]
    out_own = after(out_own, dn1_run)
    out_pieces = [out_own[:, s * local : (s + 1) * local] for s in range(count)]
    out_pieces = exchange(out_pieces, 1)
    out_weight_grad = jnp.transpose(plus(*out_pieces))
    y_run = plus(after(y_run, *out_pieces[1:]), ys[count - 1]).astype(BF)
    y_run = shift(y_run, count, 1)

    for b in range(lax.axis_size("fsdp").bit_length() - 1):
        packed = across(after(packed, part, *out_pieces[1:]) if b == 0 else packed, "fsdp", 1 << b)

    def expert_out(owns, axes):
        shaped = [own.reshape(own.shape[0], each, ff) for own in owns]
        return jnp.concatenate([jnp.transpose(v, axes) for v in shaped], axis=0).astype(F32)

    wide = each * ff
    gate_grad = expert_out((first_own[:, :wide], last_own[:, :wide]), (1, 0, 2))
    up_grad = expert_out((first_own[:, wide : 2 * wide], last_own[:, wide:]), (1, 0, 2))
    down_grad = expert_out((first_own[:, 2 * wide :], rest_own[:, :wide]), (1, 2, 0))

    attn_back = norm_back(dn1, tok_float, attn_gain)[0]
    tokens_grad = attn_back + dx1
    y_run = after(y_run, tokens_grad, out_weight_grad)
    layer_out = (x1 + plus(y_run, ys[0])).astype(BF)

    split = depth * EXPERTS // LANES
    across = depth // LANES
    small = (
        packed[split : split + across].reshape(depth),
        packed[split + 2 * across],
        packed[split + 2 * across + 1],
        packed[split + across : split + 2 * across].reshape(depth),
        packed[:split].reshape(depth, EXPERTS),
    )
    router_rows = depth // lax.axis_size("fsdp")
    router_grad = lax.dynamic_slice_in_dim(
        small[4], lax.axis_index("fsdp") * router_rows, router_rows, 0
    )

    def back_to_positions(value):
        return jnp.transpose(value.reshape(seqs, per, depth), (1, 0, 2))

    return (
        back_to_positions(layer_out),
        back_to_positions(tokens_grad),
        small[0],
        small[1],
        small[2],
        qkv_sum[:, :local],
        qkv_sum[:, local : 2 * local],
        qkv_sum[:, 2 * local :],
        out_weight_grad,
        small[3],
        router_grad,
        gate_grad,
        up_grad,
        down_grad,
    )


def solution(mesh):
    return jax.shard_map(
        per_device,
        mesh=mesh,
        in_specs=(
            P("tp", "fsdp", None),
            P("fsdp"),
            P("tp", "fsdp", None),
            P("tp", "fsdp", None),
            P(),
            P(),
            P(),
            P("fsdp", "tp"),
            P("fsdp", "tp"),
            P("fsdp", "tp"),
            P("tp", "fsdp"),
            P(),
            P("fsdp", None),
            P(None, "fsdp", "tp"),
            P(None, "fsdp", "tp"),
            P(None, "tp", "fsdp"),
            P("tp", "fsdp", None),
        ),
        out_specs=(
            P("tp", "fsdp", None),
            P("tp", "fsdp", None),
            P(),
            P(),
            P(),
            P("fsdp", "tp"),
            P("fsdp", "tp"),
            P("fsdp", "tp"),
            P("tp", "fsdp"),
            P(),
            P("fsdp", None),
            P(None, "fsdp", "tp"),
            P(None, "fsdp", "tp"),
            P(None, "tp", "fsdp"),
        ),
        check_vma=False,
    )
```

```python
import functools

import jax
import jax.numpy as jnp
from jax import lax
from jax.experimental import pallas as pl
from jax.experimental.pallas import tpu as pltpu
from jax.sharding import PartitionSpec as P

EXPERTS = 16
TOP = 8
CAP = 1280
LANES = 128

EPS = 1e-06
ROPE_BASE = 10000.0
NEG_FILL = -1e30
FAR = 1 << 20
BF = jnp.bfloat16
F32 = jnp.float32
VMEM_BYTES = 58 * 1024 * 1024
GROUPS = 2


def dot_nn(a, b):
    return lax.dot_general(a, b, (((1,), (0,)), ((), ())), preferred_element_type=F32)


def dot_nt(a, b):
    return lax.dot_general(a, b, (((1,), (1,)), ((), ())), preferred_element_type=F32)


def dot_tn(a, b):
    return lax.dot_general(a, b, (((0,), (0,)), ((), ())), preferred_element_type=F32)


def params(steps):
    return pltpu.CompilerParams(
        dimension_semantics=("arbitrary",) * steps, vmem_limit_bytes=VMEM_BYTES
    )


def cost(macs, nbytes, exps=0):
    return pl.CostEstimate(flops=32 * macs, bytes_accessed=nbytes, transcendentals=exps)


def struct(shape, dtype):
    return jax.ShapeDtypeStruct(shape, dtype)


def rms_scale(values):
    return lax.rsqrt(jnp.mean(values * values, axis=-1, keepdims=True) + EPS)


def norm_back(grad_in, raw_values, gain_values):
    scale_rows = rms_scale(raw_values)
    normed = raw_values * scale_rows
    scaled = grad_in * gain_values
    grad_raw = scale_rows * (scaled - normed * jnp.mean(scaled * normed, axis=-1, keepdims=True))
    grad_gain = jnp.sum(grad_in * normed, axis=tuple(range(grad_in.ndim - 1)))
    return (grad_raw, grad_gain)


def shift(value, count, step):
    return lax.ppermute(value, "tp", [(i, (i + step) % count) for i in range(count)])


def after(value, *done):
    return lax.optimization_barrier((value,) + done)[0]


def exchange(parts, step):
    return [parts[0]] + [shift(parts[s], len(parts), s * step) for s in range(1, len(parts))]


def plus(arrived, *parts):
    total = arrived.astype(F32)
    for part in parts:
        total = total + part.astype(F32)
    return total


def keep_kernel(bits, order_ref, keep_ref):
    count, experts, rows = order_ref.shape

    def below(limit):
        found = jnp.zeros((experts, 1), jnp.int32)
        for k in range(count):
            found = found + jnp.sum(
                (order_ref[k] < limit).astype(jnp.int32), axis=1, keepdims=True
            )
        return found

    last = jnp.zeros((experts, 1), jnp.int32)
    for bit in range(bits - 1, -1, -1):
        trial = last + (1 << bit)
        last = jnp.where(below(trial) < CAP, trial, last)
    for k in range(count):
        keep = (order_ref[k] <= last).astype(F32)
        wide = jnp.concatenate([keep, jnp.zeros((LANES - experts, rows), F32)], axis=0)
        keep_ref[k] = wide.T


def keep_rows(order_all, pair_count):
    count, experts, rows = order_all.shape
    return pl.pallas_call(
        functools.partial(keep_kernel, pair_count.bit_length() + 1),
        out_shape=struct((count, rows, LANES), F32),
        compiler_params=pltpu.CompilerParams(vmem_limit_bytes=VMEM_BYTES),
        cost_estimate=cost(16 * count * experts * rows, count * rows * LANES * 4),
        name="keep_rows",
    )(order_all)


def qkv_kernel(seqs, x_ref, wq_ref, wk_ref, wv_ref, cos_ref, sin_ref, gq_ref, gk_ref, *rest):
    qr_ref, kr_ref, q_ref, k_ref, v_ref = rest[-5:]
    rows = x_ref.shape[0] // seqs
    width = wq_ref.shape[1]
    heads = width // LANES
    x = x_ref[...]
    for w_ref, raw_ref, low_ref, gain_ref in (
        (wq_ref, qr_ref, q_ref, gq_ref),
        (wk_ref, kr_ref, k_ref, gk_ref),
    ):
        raw = dot_nn(x, w_ref[...])
        for s in range(seqs):
            for h in range(heads):
                part = raw[s * rows : (s + 1) * rows, h * LANES : (h + 1) * LANES]
                raw_ref[0, s, :, h * LANES : (h + 1) * LANES] = part
                normed = part * rms_scale(part) * gain_ref[...]
                turned = normed * cos_ref[0] + pltpu.roll(normed, LANES // 2, 1) * sin_ref[0]
                low_ref[0, s, :, h * LANES : (h + 1) * LANES] = turned.astype(BF)
    value = dot_nn(x, wv_ref[...]).astype(BF)
    for s in range(seqs):
        v_ref[0, s] = value[s * rows : (s + 1) * rows]


def project(k, count, seqs, x, weights, cos, sin, gain_q, gain_k, kept):
    rows, depth = x.shape
    local = (weights.shape[1] - LANES) // 3
    group = min(256, local)
    groups = local // group
    per = rows // seqs
    const = lambda *shape: pl.BlockSpec(shape, lambda g: (0,) * len(shape))
    table = pl.BlockSpec((1, per, LANES), lambda g: (k, 0, 0))
    out = pl.BlockSpec((1, seqs, per, group), lambda g: (k, 0, 0, g))
    shapes = [struct((count, seqs, per, local), d) for d in (F32, F32, BF, BF, BF)]
    aliased = list(kept or ())
    return pl.pallas_call(
        functools.partial(qkv_kernel, seqs),
        grid=(groups,),
        in_specs=[
            const(rows, depth),
            pl.BlockSpec((depth, group), lambda g: (0, g)),
            pl.BlockSpec((depth, group), lambda g: (0, groups + g)),
            pl.BlockSpec((depth, group), lambda g: (0, 2 * groups + g)),
            table,
            table,
            const(1, LANES),
            const(1, LANES),
        ]
        + [pl.BlockSpec(memory_space=pl.ANY)] * len(aliased),
        out_specs=[out] * 5,
        out_shape=shapes,
        input_output_aliases={8 + i: i for i in range(len(aliased))},
        compiler_params=params(1),
        cost_estimate=cost(rows * depth * local * 3 // 16, rows * depth * 2 + depth * local * 6),
        name="project",
    )(x, weights, weights, weights, cos, sin, gain_q, gain_k, *aliased)


def attend_kernel(scale, q_ref, k_ref, v_ref, valid_ref, o_ref, lse_ref):
    count, _, rows, width = q_ref.shape
    length = count * rows
    keys = k_ref[...].reshape(length, width)
    values_t = v_ref[...].reshape(length, width).astype(F32).T.astype(BF)
    valid = valid_ref[0][:, :1] > 0
    for i in range(count):
        scores = dot_nt(keys, q_ref[i, 0]) * scale
        weights = jnp.exp(jnp.where(valid, scores, NEG_FILL))
        total = jnp.sum(weights, axis=0, keepdims=True)
        out_t = dot_nn(values_t, weights.astype(BF)) / total
        o_ref[i, 0] = out_t.T.astype(BF)
        lse_ref[0, i : i + 1, :] = jnp.log(total)


def attend(q, k, v, valid, scale):
    count, seqs, rows, local = q.shape
    heads = local // LANES
    head = pl.BlockSpec((count, 1, rows, LANES), lambda s, h: (0, s, 0, h))
    return pl.pallas_call(
        functools.partial(attend_kernel, scale),
        grid=(seqs, heads),
        in_specs=[head, head, head, pl.BlockSpec((1, count * rows, LANES), lambda s, h: (s, 0, 0))],
        out_specs=[head, pl.BlockSpec((1, count, rows), lambda s, h: (s * heads + h, 0, 0))],
        out_shape=[struct(q.shape, BF), struct((seqs * heads, count, rows), F32)],
        compiler_params=params(2),
        cost_estimate=cost(
            2 * seqs * local * (count * rows) ** 2,
            4 * count * seqs * rows * local * 2,
            seqs * heads * (count * rows) ** 2,
        ),
        name="attend",
    )(q, k, v, valid)


def attend_back_kernel(scale, *refs):
    q_ref, k_ref, v_ref, o_ref, lse_ref, valid_ref = refs[:6]
    qr_ref, kr_ref, cos_ref, sin_ref, gq_ref, gk_ref = refs[6:12]
    do_refs = refs[12:-6]
    dq_ref, dk_ref, dv_ref, gains_ref, dk_acc, dv_acc = refs[-6:]
    count, _, rows, width = q_ref.shape
    length = count * rows
    first = jnp.logical_and(pl.program_id(0) == 0, pl.program_id(1) == 0)

    @pl.when(first)
    def _():
        gains_ref[...] = jnp.zeros_like(gains_ref)

    keys = k_ref[...].reshape(length, width)
    keys_t = keys.astype(F32).T.astype(BF)
    values = v_ref[...].reshape(length, width)
    valid = valid_ref[0][:, :1] > 0
    ones = jnp.ones((8, width), F32)

    def back(grad, raw, cos, sin, gain):
        turned = grad * cos - pltpu.roll(grad, LANES // 2, 1) * sin
        scale_rows = rms_scale(raw)
        normed = raw * scale_rows
        scaled = turned * gain
        mean = jnp.mean(scaled * normed, axis=-1, keepdims=True)
        return scale_rows * (scaled - normed * mean), jnp.sum(
            turned * normed, axis=0, keepdims=True
        )

    gain_q = jnp.zeros((1, width), F32)
    gain_k = jnp.zeros((1, width), F32)
    for i in range(count):
        query = q_ref[i, 0]
        grad = do_refs[i][0]
        scores = dot_nt(keys, query) * scale
        weights = jnp.exp(jnp.where(valid, scores, NEG_FILL) - lse_ref[0, i : i + 1, :])
        delta = jnp.sum(
            (grad.astype(F32) * o_ref[i, 0].astype(F32)).T, axis=0, keepdims=True
        )
        d_weights = dot_nt(values, grad)
        d_scores = (weights * (d_weights - delta)).astype(BF)
        dv_part = dot_nn(weights.astype(BF), grad)
        dk_part = dot_nn(d_scores, query)
        if i == 0:
            dv_acc[...] = dv_part
            dk_acc[...] = dk_part
        else:
            dv_acc[...] += dv_part
            dk_acc[...] += dk_part
        dq = (dot_nn(keys_t, d_scores) * scale).T
        d_raw, d_gain = back(dq, qr_ref[i, 0], cos_ref[i], sin_ref[i], gq_ref[...])
        gain_q = gain_q + d_gain
        dq_ref[i, 0] = d_raw.astype(BF)
    for i in range(count):
        dv_ref[i, 0] = dv_acc[i * rows : (i + 1) * rows].astype(BF)
        dk = dk_acc[i * rows : (i + 1) * rows] * scale
        d_raw, d_gain = back(dk, kr_ref[i, 0], cos_ref[i], sin_ref[i], gk_ref[...])
        gain_k = gain_k + d_gain
        dk_ref[i, 0] = d_raw.astype(BF)
    gains_ref[0:1, :] += gain_q
    gains_ref[1:2, :] += gain_k


def attend_back(q, k, v, o, do, lse, valid, q_raw, k_raw, cos, sin, gain_q, gain_k, scale):
    count, seqs, rows, local = q.shape
    heads = local // LANES
    head = pl.BlockSpec((count, 1, rows, LANES), lambda s, h: (0, s, 0, h))
    const = lambda *shape: pl.BlockSpec(shape, lambda s, h: (0,) * len(shape))
    return pl.pallas_call(
        functools.partial(attend_back_kernel, scale),
        grid=(seqs, heads),
        in_specs=[
            head,
            head,
            head,
            head,
            pl.BlockSpec((1, count, rows), lambda s, h: (s * heads + h, 0, 0)),
            pl.BlockSpec((1, count * rows, LANES), lambda s, h: (s, 0, 0)),
            head,
            head,
            const(count, rows, LANES),
            const(count, rows, LANES),
            const(1, LANES),
            const(1, LANES),
        ]
        + [pl.BlockSpec((1, rows, LANES), lambda s, h: (s, 0, h))] * count,
        out_specs=[head, head, head, const(8, LANES)],
        out_shape=[struct(q.shape, BF)] * 3 + [struct((8, LANES), F32)],
        scratch_shapes=[pltpu.VMEM((count * rows, LANES), F32)] * 2,
        compiler_params=params(2),
        cost_estimate=cost(
            5 * seqs * local * (count * rows) ** 2,
            12 * count * seqs * rows * local * 2,
            seqs * heads * (count * rows) ** 2,
        ),
        name="attend_back",
    )(q, k, v, o, lse, valid, q_raw, k_raw, cos, sin, gain_q, gain_k, *do)


def input_back_kernel(dq_ref, dk_ref, dv_ref, wq_ref, wk_ref, wv_ref, out_ref):
    total = None
    for d_ref, w_ref in ((dq_ref, wq_ref), (dk_ref, wk_ref), (dv_ref, wv_ref)):
        grad = d_ref[0].reshape(out_ref.shape[0], w_ref.shape[1])
        part = dot_nt(grad, w_ref[...])
        total = part if total is None else total + part
    out_ref[...] = total.astype(BF)


def input_back(k, dq, dk, dv, weights):
    _, seqs, per, local = dq.shape
    depth = weights.shape[0]
    rows = seqs * per
    tile = min(512, depth)
    grad = pl.BlockSpec((1, seqs, per, local), lambda t: (k, 0, 0, 0))
    return pl.pallas_call(
        input_back_kernel,
        grid=(depth // tile,),
        in_specs=[grad] * 3
        + [pl.BlockSpec((tile, local), lambda t, j=j: (t, j)) for j in range(3)],
        out_specs=pl.BlockSpec((rows, tile), lambda t: (0, t)),
        out_shape=struct((rows, depth), BF),
        compiler_params=params(1),
        cost_estimate=cost(rows * depth * local * 3 // 16, rows * depth * 2 + depth * local * 6),
        name="input_back",
    )(dq, dk, dv, weights, weights, weights)


def out_kernel(count, tok_ref, *refs):
    ob_refs = refs[:count]
    w_ref, x1_ref = refs[count:]
    local = ob_refs[0].shape[1]
    total = tok_ref[...].astype(F32)
    for s in range(count):
        total = total + dot_nn(ob_refs[s][...], w_ref[0, s * local : (s + 1) * local, :])
    x1_ref[...] = total


def out_project(tok, parts, weights):
    rows, depth = tok.shape
    blocks, full, tile = weights.shape
    count = len(parts)
    return pl.pallas_call(
        functools.partial(out_kernel, count),
        grid=(blocks,),
        in_specs=[pl.BlockSpec((rows, tile), lambda j: (0, j))]
        + [pl.BlockSpec(parts[0].shape, lambda j: (0, 0))] * count
        + [pl.BlockSpec((1, full, tile), lambda j: (j, 0, 0))],
        out_specs=pl.BlockSpec((rows, tile), lambda j: (0, j)),
        out_shape=struct((rows, depth), F32),
        compiler_params=params(1),
        cost_estimate=cost(rows * depth * full, rows * depth * 8 + full * depth * 2),
        name="out_project",
    )(tok, *parts, weights)


def out_back_kernel(db_ref, w_ref, out_ref):
    blocks, _, tile = w_ref.shape
    total = None
    for j in range(blocks):
        part = dot_nt(db_ref[:, j * tile : (j + 1) * tile], w_ref[j])
        total = part if total is None else total + part
    out_ref[0] = total.astype(BF)


def out_back(db, weights, count):
    rows, depth = db.shape
    blocks, full, tile = weights.shape
    local = full // count
    return pl.pallas_call(
        out_back_kernel,
        grid=(count,),
        in_specs=[
            pl.BlockSpec((rows, depth), lambda s: (0, 0)),
            pl.BlockSpec((blocks, local, tile), lambda s: (0, s, 0)),
        ],
        out_specs=pl.BlockSpec((1, rows, local), lambda s: (s, 0, 0)),
        out_shape=struct((count, rows, local), BF),
        compiler_params=params(1),
        cost_estimate=cost(rows * depth * full, rows * depth * 2 + full * depth * 2),
        name="out_back",
    )(db, weights)


def expert_kernel(group, experts, n2_ref, c_ref, keep_ref, router_ref, tile_ref, w_ref, *rest):
    last = group == GROUPS - 1
    wt_ref, grad_in, y_in, dn_in = rest[:4]
    hp_ref, da_ref, du_ref, y_ref, dn_ref, grad_out = rest[-14:-8]
    probs, gates, grads, hp_all, da_all, du_all, full, low = rest[-8:]
    e = pl.program_id(0)
    blocks, _, _, ff, tile = w_ref.shape
    rows = n2_ref.shape[0]
    lane = lax.broadcasted_iota(jnp.int32, (rows, LANES), 1)

    @pl.when(e == 0)
    def _():
        logits = jnp.where(lane < EXPERTS, dot_nn(n2_ref[...], router_ref[...]), NEG_FILL)
        raised = jnp.exp(logits - jnp.max(logits, axis=-1, keepdims=True))
        soft = raised / jnp.sum(raised, axis=-1, keepdims=True)
        probs[...] = soft
        gates[...] = soft * keep_ref[0]
        grads[...] = jnp.zeros_like(grads) if group == 0 else grad_in[...]

    @pl.when(e < experts)
    def _():
        for t in range(3):
            for j in range(blocks):
                full[t, :, j * tile : (j + 1) * tile] = w_ref[j, t, 0]
        here = lane == e + group * experts
        gate = jnp.sum(jnp.where(here, gates[...], 0.0), axis=-1, keepdims=True)
        x = n2_ref[...]
        pre = dot_nt(x, full[0])
        up = dot_nt(x, full[1])
        back = dot_nt(c_ref[...], full[2])
        sig = 1.0 / (1.0 + jnp.exp(-pre))
        act = pre * sig
        hid = act * up
        hp = (hid * gate).astype(BF)
        column = jnp.sum(back * hid, axis=-1, keepdims=True)
        grads[...] += jnp.where(here, column * keep_ref[0], 0.0)
        dh = back * gate
        du = (dh * act).astype(BF)
        da = (dh * up * (sig + act * (1.0 - sig))).astype(BF)
        hp_ref[0] = hp
        da_ref[0] = da
        du_ref[0] = du
        place = pl.ds(pl.multiple_of(e * ff, ff), ff)
        hp_all[:, place] = hp
        da_all[:, place] = da
        du_all[:, place] = du

    @pl.when(e == experts - 1)
    def _():
        if last:
            soft = probs[...]
            gd = grads[...]
            dl = (soft * (gd - jnp.sum(soft * gd, axis=-1, keepdims=True))).astype(BF)
            grad_out[...] = dl
            low[...] = dl
        else:
            grad_out[...] = grads[...]

    @pl.when(e >= experts)
    def _():
        wide = experts * ff
        y = dot_nn(hp_all[...], wt_ref[0, 2].reshape(wide, tile))
        total = dot_nn(da_all[...], wt_ref[0, 0].reshape(wide, tile))
        total = total + dot_nn(du_all[...], wt_ref[0, 1].reshape(wide, tile))
        if last:
            total = total + dot_nt(low[...], tile_ref[...])
        if group > 0:
            y = y + y_in[...].astype(F32)
            total = total + dn_in[...].astype(F32)
        y_ref[...] = y.astype(BF)
        dn_ref[...] = total.astype(BF)


def experts_pass(k, count, group, n2, cot, keep, weights_all, weights, before, kept):
    rows, depth = n2.shape
    blocks, _, experts, ff, tile = weights.shape
    router_col = weights_all.shape[1] // LANES - 1
    const = lambda *shape: pl.BlockSpec(shape, lambda e: (0,) * len(shape))
    near = lambda e: jnp.minimum(e, experts - 1)
    far = lambda e: jnp.maximum(e - experts, 0)
    wide = pl.BlockSpec((1, rows, ff), lambda e: (k, 0, near(e)))
    part = pl.BlockSpec((rows, tile), lambda e: (0, far(e)))
    aliased = list(kept or ())
    grad, *sums = before or (jnp.zeros((8, LANES), F32),)
    return pl.pallas_call(
        functools.partial(expert_kernel, group, experts),
        grid=(experts + blocks,),
        in_specs=[
            const(rows, depth),
            const(rows, depth),
            pl.BlockSpec((1, rows, LANES), lambda e: (k, 0, 0)),
            pl.BlockSpec((depth, LANES), lambda e: (0, router_col)),
            pl.BlockSpec((tile, LANES), lambda e: (far(e), router_col)),
            pl.BlockSpec((blocks, 3, 1, ff, tile), lambda e: (0, 0, near(e), 0, 0)),
            pl.BlockSpec((1, 3, experts, ff, tile), lambda e: (far(e), 0, 0, 0, 0)),
            const(*grad.shape),
        ]
        + [part] * len(sums)
        + [pl.BlockSpec(memory_space=pl.ANY)] * len(aliased),
        out_specs=[wide, wide, wide, part, part, const(rows, LANES)],
        out_shape=[struct((count, rows, experts * ff), BF)] * 3
        + [struct((rows, depth), BF)] * 2
        + [struct((rows, LANES), BF if group == GROUPS - 1 else F32)],
        input_output_aliases={8 + len(sums) + i: i for i in range(len(aliased))},
        scratch_shapes=[pltpu.VMEM((rows, LANES), F32)] * 3
        + [pltpu.VMEM((rows, experts * ff), BF)] * 3
        + [pltpu.VMEM((3, ff, depth), BF), pltpu.VMEM((rows, LANES), BF)],
        compiler_params=params(1),
        cost_estimate=cost(
            6 * rows * depth * ff * experts,
            6 * experts * depth * ff * 2 + 4 * rows * depth * 2 + 3 * rows * experts * ff * 2,
            2 * rows * ff * experts,
        ),
        name=f"experts_{group}",
    )(n2, cot, keep, weights_all, weights_all, weights, weights, grad, *sums, *aliased)


def row_grad_kernel(count, plan, router, gain, shared, *refs):
    ins = list(refs)
    lefts, rights = [], []
    for parts, tiles in plan:
        lefts.append([ins.pop(0) for _ in range(parts)])
        rights.append([ins.pop(0) for _ in tiles])
    dls = [ins.pop(0) for _ in range(count)] if router else []
    weight_ref = ins.pop(0) if gain else None
    if shared:
        ins.pop(0)
    out_ref, extra_ref, turned = ins.pop(0), ins.pop(0) if router or gain else None, ins.pop(0)
    i = pl.program_id(0)
    start = 0
    for (parts, tiles), left, right in zip(plan, lefts, rights):
        rows = left[0].shape[0]

        @pl.when(i == start)
        def _():
            for k in range(parts):
                turned[:, k * rows : (k + 1) * rows] = left[k][...].T
            if router and start == 0:
                total = None
                for k in range(count):
                    part = dot_nn(turned[:, k * rows : (k + 1) * rows], dls[k][...])
                    total = part if total is None else total + part
                extra_ref[...] = total
            if gain:
                extra_ref[...] = jnp.zeros_like(extra_ref)

        for ref, steps in zip(right, tiles):

            @pl.when(jnp.logical_and(i >= start, i < start + steps))
            def _():
                tile = out_ref.shape[1]
                full = dot_nn(turned[:, : parts * rows], ref[...].reshape(parts * rows, tile))
                out_ref[...] = full.astype(BF)
                if gain:
                    product = full * weight_ref[...].astype(F32)
                    for j in range(tile // LANES):
                        extra_ref[...] += product[:, j * LANES : (j + 1) * LANES]

            start += steps


def row_grads(pairs, tile, name, dls=(), weights=None, total=None, base=None):
    plan, args, specs, start, macs = [], [], [], 0, 0
    depth = pairs[0][0][0].shape[1]
    most = max(sum(part.shape[0] for part in left) for left, _ in pairs)

    def piece(array, first, steps):
        lead = array.shape[:-1]
        return pl.BlockSpec(
            lead + (tile,),
            lambda i: (0,) * len(lead) + (jnp.clip(i - first, 0, steps - 1),),
        )

    whole = pl.Buffered(1)
    for left, right in pairs:
        args += left
        specs += [pl.BlockSpec(p.shape, lambda i: (0, 0), pipeline_mode=whole) for p in left]
        tiles = []
        for array in right:
            steps = array.shape[-1] // tile
            args.append(array)
            specs.append(piece(array, start, steps))
            tiles.append(steps)
            start += steps
            macs += len(left) * left[0].shape[0] * depth * steps * tile
        plan.append((len(left), tuple(tiles)))
    wide = base.shape[1] if base is not None else total or start * tile
    skip = wide // tile - start if base is not None else 0
    out_specs = [pl.BlockSpec((depth, tile), lambda i: (0, i + skip))]
    out_shape = [struct((depth, wide), BF)]
    if dls:
        args += dls
        specs += [pl.BlockSpec(d.shape, lambda i: (0, 0)) for d in dls]
    if weights is not None:
        args.append(weights)
        specs.append(pl.BlockSpec((depth, tile), lambda i: (0, i)))
    if base is not None:
        args.append(base)
        specs.append(pl.BlockSpec(memory_space=pl.ANY))
    if dls or weights is not None:
        out_specs.append(pl.BlockSpec((depth, LANES), lambda i: (0, 0)))
        out_shape.append(struct((depth, LANES), F32))
    return pl.pallas_call(
        functools.partial(
            row_grad_kernel,
            len(dls),
            tuple(plan),
            bool(dls),
            weights is not None,
            base is not None,
        ),
        grid=(start,),
        in_specs=specs,
        out_specs=out_specs,
        out_shape=out_shape,
        scratch_shapes=[pltpu.VMEM((depth, most), BF)],
        input_output_aliases={} if base is None else {len(args) - 1: 0},
        compiler_params=params(1),
        cost_estimate=cost(macs if 'experts' in name else macs // 16, 2 * depth * start * tile + 4 * most * depth),
        name=name,
    )(*args)


def per_device(
    tokens,
    lengths,
    routes,
    slot_order,
    attn_gain,
    query_gain,
    key_gain,
    query_weight,
    key_weight,
    value_weight,
    out_weight,
    moe_gain,
    router_weight,
    gate_weight,
    up_weight,
    down_weight,
    cotangent,
):
    per, seqs, depth = tokens.shape
    count = lax.axis_size("tp")
    me = lax.axis_index("tp")
    length = per * count
    rows = seqs * per
    head_width = query_gain.shape[0]
    local = query_weight.shape[1]
    scale = head_width ** (-0.5)

    first = jnp.concatenate(
        [
            query_weight,
            key_weight,
            value_weight,
            jnp.pad(router_weight, ((0, 0), (0, LANES - EXPERTS))),
        ],
        axis=1,
    )
    weights_all = lax.all_gather(first, "fsdp", axis=0, tiled=True)

    tok = jnp.transpose(tokens, (1, 0, 2)).reshape(rows, depth)
    tok_float = tok.astype(F32)
    n1_own = (tok_float * rms_scale(tok_float) * attn_gain).astype(BF)
    outs = exchange([after(out_weight, n1_own)] * count, -1)
    n1 = [n1_own, shift(after(n1_own, *outs[1:]), count, 1)]
    own_pos = me * per + jnp.arange(per, dtype=jnp.int32)
    valid_own = own_pos[None, :] < lengths[:, None]
    route_t = jnp.transpose(routes, (2, 1, 0)).reshape(TOP, rows)
    order_t = jnp.transpose(slot_order, (2, 1, 0)).reshape(TOP, rows)
    names = jnp.arange(EXPERTS, dtype=jnp.int32)[:, None]
    order_own = jnp.full((EXPERTS, rows), FAR, jnp.int32)
    for j in range(TOP):
        order_own = jnp.where(route_t[j][None, :] == names, order_t[j][None, :], order_own)
    order_own = jnp.where(valid_own.reshape(1, rows), order_own, FAR)
    orders = exchange([after(order_own, n1[1])] * count, 1)

    each = EXPERTS // GROUPS
    gather = lambda value: lax.all_gather(value, "fsdp", axis=0, tiled=False)

    def group_weights(g):
        part = slice(g * each, (g + 1) * each)
        stacked = jnp.concatenate(
            [
                jnp.swapaxes(gate_weight[part], 1, 2),
                jnp.swapaxes(up_weight[part], 1, 2),
                down_weight[part],
            ]
        )
        stacked = after(stacked, weights_all, n1[1])
        return gather(stacked.reshape((3, each) + stacked.shape[1:]))

    out_all = gather(jnp.concatenate(outs, axis=0))
    moe_weights = [group_weights(g) for g in range(GROUPS)]
    owner = (me - jnp.arange(count, dtype=jnp.int32)) % count
    chunk_pos = owner[:, None] * per + jnp.arange(per, dtype=jnp.int32)[None, :]
    half = head_width // 2
    frequency = ROPE_BASE ** (-(jnp.arange(half, dtype=F32) * 2.0 / head_width))
    angles = chunk_pos.astype(F32)[:, :, None] * frequency
    cos_half, sin_half = jnp.cos(angles), jnp.sin(angles)
    cos = jnp.concatenate([cos_half, cos_half], axis=-1)
    sin = jnp.concatenate([-sin_half, sin_half], axis=-1)
    key_valid = (chunk_pos.reshape(1, length) < lengths[:, None]).astype(F32)
    key_valid = jnp.broadcast_to(key_valid[:, :, None], (seqs, length, LANES))

    gain_q, gain_k = query_gain[None, :], key_gain[None, :]
    kept, done = None, []
    for k in range(count):
        if k > 1:
            n1.append(shift(after(n1[-1], *(done[: k - 1] if k > 2 else ())), count, 1))
        kept = project(
            k, count, seqs, after(n1[k], *done[-1:]), weights_all, cos, sin, gain_q, gain_k, kept
        )
        done.append(kept[4])
    q_raw, k_raw, q, k_low, v = kept
    keep = keep_rows(after(jnp.stack(orders), done[1]), length * seqs * TOP)

    cot = jnp.transpose(cotangent, (1, 0, 2)).reshape(rows, depth)
    cot_own = jnp.where(valid_own.reshape(rows, 1), cot, jnp.zeros_like(cot))
    cots = [cot_own, shift(after(cot_own, n1[-1], done[count - 2]), count, 1)]

    ob, lse = attend(q, k_low, v, key_valid, scale)
    ob_rows = after(ob.reshape(count, rows, local), cots[1])
    ob_parts = exchange(ob_rows, -1)
    x1 = out_project(tok, ob_parts, out_all)
    n2_own = (x1 * rms_scale(x1) * moe_gain).astype(BF)
    n2 = [n2_own, shift(n2_own, count, 1)]
    token = [n2_own]

    bufs = [None] * GROUPS
    ys, dns, grads = [None] * count, [None] * count, [None] * count

    def run(group, k):
        before = (grads[k], ys[k], dns[k]) if group else None
        hp, da, du, ys[k], dns[k], grads[k] = experts_pass(
            k, count, group, after(n2[k], *token), cots[k], keep, weights_all, moe_weights[group],
            before, bufs[group],
        )
        bufs[group] = (hp, da, du)
        token[0] = dns[k]
        return dns[k]

    def next_inputs(done):
        if len(n2) < count:
            n2.append(shift(after(n2[-1], done), count, 1))
        if len(cots) < count:
            cots.append(shift(after(cots[-1], done), count, 1))

    ready = run(0, 0)
    next_inputs(ready)
    run(0, 1)
    ready = run(1, 0)
    next_inputs(ready)
    for k in range(2, count):
        run(0, k)
        if k < count - 1:
            next_inputs(run(1, k - 1))
    dn_run = shift(dns[1], count, 1)
    token.append(dn_run)
    y_run = shift(after(ys[1], dns[count - 1]), count, 1)
    ff = gate_weight.shape[2]
    hp, da, du = bufs[0]
    first_full = row_grads(
        [([after(n2[0], *token)] + n2[1:], [da, du]), (cots, [hp])], ff, "experts_first_grads"
    )[0]
    first_own = lax.psum_scatter(first_full, "fsdp", scatter_dimension=0, tiled=True)
    token = [first_full, y_run]
    run(1, count - 2)
    for k in range(2, count):
        dn_run = plus(dn_run, dns[k]).astype(BF)
        token.append(dn_run)
        if k == count - 2:
            run(1, count - 1)
        dn_run = shift(dn_run, count, 1)
    hp, da, du = bufs[1]
    last_full, router_term = row_grads(
        [([after(n2[0], *token)] + n2[1:], [da, du])], ff, "experts_last_grads", grads
    )
    dn2 = plus(after(dn_run, last_full), dns[0])


    moe_back, moe_gain_term = norm_back(dn2, x1, moe_gain)
    dx1 = moe_back + cot_own.astype(F32)
    db = dx1.astype(BF)
    dob = out_back(db, out_all, count)
    last_own = lax.psum_scatter(after(last_full, dob), "fsdp", scatter_dimension=0, tiled=True)
    dob = after(dob, first_own)
    dob_parts = exchange(dob, 1)
    y_sum = plus(after(y_run, dob), ys[2]).astype(BF)
    rest_full = row_grads(
        [(cots, [hp]), ([after(db, dob)], ob_parts)],
        ff, "rest_grads",
    )[0]
    d_ob = [after(part.reshape(seqs, per, local), rest_full, y_sum) for part in dob_parts]
    rest_own = lax.psum_scatter(after(rest_full, *d_ob), "fsdp", scatter_dimension=0, tiled=True)
    y_run = shift(after(y_sum, *d_ob), count, 1)
    for k in range(3, count - 1):
        y_run = shift(plus(y_run, ys[k]).astype(BF), count, 1)

    dq, dk, dv, gains = attend_back(
        q, k_low, v, ob, d_ob, lse, key_valid, q_raw, k_raw, cos, sin, gain_q, gain_k, scale
    )
    part = input_back(1, after(dq, y_run), dk, dv, weights_all)
    dn1_run = shift(part, count, 1)
    attn_full, attn_gain_wide = row_grads(
        [([after(n1[0], part)] + n1[1:], [a.reshape(count * rows, local) for a in (dq, dk, dv)])],
        min(256, local), "qkv_grads", weights=weights_all,
    )

    attn_own = lax.psum_scatter(attn_full, "fsdp", scatter_dimension=0, tiled=True)

    attn_gain_term = jnp.sum(attn_gain_wide, axis=1) / attn_gain
    packed = jnp.concatenate(
        [router_term[:, :EXPERTS].reshape(-1, LANES)]
        + [v.reshape(-1, LANES) for v in (attn_gain_term, moe_gain_term, gains[:2])],
        axis=0,
    )
    bits = [1 << b for b in range(count.bit_length() - 1)]
    across = lambda value, axis, bit: value + lax.ppermute(
        value, axis, [(i, i ^ bit) for i in range(lax.axis_size(axis))]
    )

    part = input_back(2, after(dq, attn_full), dk, dv, weights_all)
    dn1_run = after(dn1_run, last_own)
    for k in range(2, count):
        dn1_run = plus(dn1_run, part).astype(BF)
        if k == 2:
            packed = after(packed, dn1_run)
            for b in range(lax.axis_size("fsdp").bit_length() - 1):
                packed = across(packed, "fsdp", 1 << b)
        elif bits:
            packed = across(after(packed, dn1_run), "tp", bits.pop())
        dn1_run = shift(dn1_run, count, 1)
        part = input_back((k + 1) % count, dq, dk, dv, weights_all)
    packed = after(packed, dn1_run)
    while bits:
        packed = across(packed, "tp", bits.pop())
    dn1 = plus(dn1_run, part)
    y_run = shift(plus(after(y_run, dn1_run, rest_own), ys[count - 1]).astype(BF), count, 1)
    qkv_sum = attn_own.astype(F32)
    out_own = rest_own[:, each * ff :]
    out_pieces = [out_own[:, s * local : (s + 1) * local] for s in range(count)]
    out_pieces = exchange(out_pieces, 1)
    out_weight_grad = jnp.transpose(plus(*out_pieces))

    def expert_out(owns, axes):
        shaped = [own.reshape(own.shape[0], each, ff) for own in owns]
        return jnp.concatenate([jnp.transpose(v, axes) for v in shaped], axis=0).astype(F32)

    wide = each * ff
    gate_grad = expert_out((first_own[:, :wide], last_own[:, :wide]), (1, 0, 2))
    up_grad = expert_out((first_own[:, wide : 2 * wide], last_own[:, wide:]), (1, 0, 2))
    down_grad = expert_out((first_own[:, 2 * wide :], rest_own[:, :wide]), (1, 2, 0))

    attn_back = norm_back(dn1, tok_float, attn_gain)[0]
    tokens_grad = attn_back + dx1
    y_run = after(y_run, tokens_grad, out_weight_grad)
    layer_out = (x1 + plus(y_run, ys[0])).astype(BF)

    split = depth * EXPERTS // LANES
    across = depth // LANES
    small = (
        packed[split : split + across].reshape(depth),
        packed[split + 2 * across],
        packed[split + 2 * across + 1],
        packed[split + across : split + 2 * across].reshape(depth),
        packed[:split].reshape(depth, EXPERTS),
    )
    router_rows = depth // lax.axis_size("fsdp")
    router_grad = lax.dynamic_slice_in_dim(
        small[4], lax.axis_index("fsdp") * router_rows, router_rows, 0
    )

    def back_to_positions(value):
        return jnp.transpose(value.reshape(seqs, per, depth), (1, 0, 2))

    return (
        back_to_positions(layer_out),
        back_to_positions(tokens_grad),
        small[0],
        small[1],
        small[2],
        qkv_sum[:, :local],
        qkv_sum[:, local : 2 * local],
        qkv_sum[:, 2 * local :],
        out_weight_grad,
        small[3],
        router_grad,
        gate_grad,
        up_grad,
        down_grad,
    )


def solution(mesh):
    return jax.shard_map(
        per_device,
        mesh=mesh,
        in_specs=(
            P("tp", "fsdp", None),
            P("fsdp"),
            P("tp", "fsdp", None),
            P("tp", "fsdp", None),
            P(),
            P(),
            P(),
            P("fsdp", "tp"),
            P("fsdp", "tp"),
            P("fsdp", "tp"),
            P("tp", "fsdp"),
            P(),
            P("fsdp", None),
            P(None, "fsdp", "tp"),
            P(None, "fsdp", "tp"),
            P(None, "tp", "fsdp"),
            P("tp", "fsdp", None),
        ),
        out_specs=(
            P("tp", "fsdp", None),
            P("tp", "fsdp", None),
            P(),
            P(),
            P(),
            P("fsdp", "tp"),
            P("fsdp", "tp"),
            P("fsdp", "tp"),
            P("tp", "fsdp"),
            P(),
            P("fsdp", None),
            P(None, "fsdp", "tp"),
            P(None, "fsdp", "tp"),
            P(None, "tp", "fsdp"),
        ),
        check_vma=False,
    )
```

```python
import functools

import jax
import jax.numpy as jnp
from jax import lax
from jax.experimental import pallas as pl
from jax.experimental.pallas import tpu as pltpu
from jax.sharding import PartitionSpec as P

EXPERTS = 16
TOP = 8
CAP = 1280
LANES = 128

EPS = 1e-06
ROPE_BASE = 10000.0
NEG_FILL = -1e30
FAR = 1 << 20
BF = jnp.bfloat16
F32 = jnp.float32
VMEM_BYTES = 58 * 1024 * 1024
GROUPS = 2


def dot_nn(a, b):
    return lax.dot_general(a, b, (((1,), (0,)), ((), ())), preferred_element_type=F32)


def dot_nt(a, b):
    return lax.dot_general(a, b, (((1,), (1,)), ((), ())), preferred_element_type=F32)


def dot_tn(a, b):
    return lax.dot_general(a, b, (((0,), (0,)), ((), ())), preferred_element_type=F32)


def params(steps):
    return pltpu.CompilerParams(
        dimension_semantics=("arbitrary",) * steps, vmem_limit_bytes=VMEM_BYTES
    )


def cost(macs, nbytes, exps=0):
    return pl.CostEstimate(flops=32 * macs, bytes_accessed=nbytes, transcendentals=exps)


def struct(shape, dtype):
    return jax.ShapeDtypeStruct(shape, dtype)


def rms_scale(values):
    return lax.rsqrt(jnp.mean(values * values, axis=-1, keepdims=True) + EPS)


def norm_back(grad_in, raw_values, gain_values):
    scale_rows = rms_scale(raw_values)
    normed = raw_values * scale_rows
    scaled = grad_in * gain_values
    grad_raw = scale_rows * (scaled - normed * jnp.mean(scaled * normed, axis=-1, keepdims=True))
    grad_gain = jnp.sum(grad_in * normed, axis=tuple(range(grad_in.ndim - 1)))
    return (grad_raw, grad_gain)


def shift(value, count, step):
    return lax.ppermute(value, "tp", [(i, (i + step) % count) for i in range(count)])


def after(value, *done):
    return lax.optimization_barrier((value,) + done)[0]


def exchange(parts, step):
    return [parts[0]] + [shift(parts[s], len(parts), s * step) for s in range(1, len(parts))]


def plus(arrived, *parts):
    total = arrived.astype(F32)
    for part in parts:
        total = total + part.astype(F32)
    return total


def keep_kernel(bits, order_ref, keep_ref):
    count, experts, rows = order_ref.shape

    def below(limit):
        found = jnp.zeros((experts, 1), jnp.int32)
        for k in range(count):
            found = found + jnp.sum(
                (order_ref[k] < limit).astype(jnp.int32), axis=1, keepdims=True
            )
        return found

    last = jnp.zeros((experts, 1), jnp.int32)
    for bit in range(bits - 1, -1, -1):
        trial = last + (1 << bit)
        last = jnp.where(below(trial) < CAP, trial, last)
    for k in range(count):
        keep = (order_ref[k] <= last).astype(F32)
        wide = jnp.concatenate([keep, jnp.zeros((LANES - experts, rows), F32)], axis=0)
        keep_ref[k] = wide.T


def keep_rows(order_all, pair_count):
    count, experts, rows = order_all.shape
    return pl.pallas_call(
        functools.partial(keep_kernel, pair_count.bit_length() + 1),
        out_shape=struct((count, rows, LANES), F32),
        compiler_params=pltpu.CompilerParams(vmem_limit_bytes=VMEM_BYTES),
        cost_estimate=cost(16 * count * experts * rows, count * rows * LANES * 4),
        name="keep_rows",
    )(order_all)


def qkv_kernel(seqs, x_ref, wq_ref, wk_ref, wv_ref, cos_ref, sin_ref, gq_ref, gk_ref, *rest):
    qr_ref, kr_ref, q_ref, k_ref, v_ref = rest[-5:]
    rows = x_ref.shape[0] // seqs
    width = wq_ref.shape[1]
    heads = width // LANES
    x = x_ref[...]
    for w_ref, raw_ref, low_ref, gain_ref in (
        (wq_ref, qr_ref, q_ref, gq_ref),
        (wk_ref, kr_ref, k_ref, gk_ref),
    ):
        raw = dot_nn(x, w_ref[...])
        for s in range(seqs):
            for h in range(heads):
                part = raw[s * rows : (s + 1) * rows, h * LANES : (h + 1) * LANES]
                raw_ref[0, s, :, h * LANES : (h + 1) * LANES] = part
                normed = part * rms_scale(part) * gain_ref[...]
                turned = normed * cos_ref[0] + pltpu.roll(normed, LANES // 2, 1) * sin_ref[0]
                low_ref[0, s, :, h * LANES : (h + 1) * LANES] = turned.astype(BF)
    value = dot_nn(x, wv_ref[...]).astype(BF)
    for s in range(seqs):
        v_ref[0, s] = value[s * rows : (s + 1) * rows]


def project(k, count, seqs, x, weights, cos, sin, gain_q, gain_k, kept):
    rows, depth = x.shape
    local = (weights.shape[1] - LANES) // 3
    group = min(256, local)
    groups = local // group
    per = rows // seqs
    const = lambda *shape: pl.BlockSpec(shape, lambda g: (0,) * len(shape))
    table = pl.BlockSpec((1, per, LANES), lambda g: (k, 0, 0))
    out = pl.BlockSpec((1, seqs, per, group), lambda g: (k, 0, 0, g))
    shapes = [struct((count, seqs, per, local), d) for d in (F32, F32, BF, BF, BF)]
    aliased = list(kept or ())
    return pl.pallas_call(
        functools.partial(qkv_kernel, seqs),
        grid=(groups,),
        in_specs=[
            const(rows, depth),
            pl.BlockSpec((depth, group), lambda g: (0, g)),
            pl.BlockSpec((depth, group), lambda g: (0, groups + g)),
            pl.BlockSpec((depth, group), lambda g: (0, 2 * groups + g)),
            table,
            table,
            const(1, LANES),
            const(1, LANES),
        ]
        + [pl.BlockSpec(memory_space=pl.ANY)] * len(aliased),
        out_specs=[out] * 5,
        out_shape=shapes,
        input_output_aliases={8 + i: i for i in range(len(aliased))},
        compiler_params=params(1),
        cost_estimate=cost(rows * depth * local * 3 // 16, rows * depth * 2 + depth * local * 6),
        name="project",
    )(x, weights, weights, weights, cos, sin, gain_q, gain_k, *aliased)


def attend_kernel(scale, q_ref, k_ref, v_ref, valid_ref, o_ref, lse_ref):
    count, _, rows, width = q_ref.shape
    length = count * rows
    keys = k_ref[...].reshape(length, width)
    values_t = v_ref[...].reshape(length, width).astype(F32).T.astype(BF)
    valid = valid_ref[0][:, :1] > 0
    for i in range(count):
        scores = dot_nt(keys, q_ref[i, 0]) * scale
        weights = jnp.exp(jnp.where(valid, scores, NEG_FILL))
        total = jnp.sum(weights, axis=0, keepdims=True)
        out_t = dot_nn(values_t, weights.astype(BF)) / total
        o_ref[i, 0] = out_t.T.astype(BF)
        lse_ref[0, i : i + 1, :] = jnp.log(total)


def attend(q, k, v, valid, scale):
    count, seqs, rows, local = q.shape
    heads = local // LANES
    head = pl.BlockSpec((count, 1, rows, LANES), lambda s, h: (0, s, 0, h))
    return pl.pallas_call(
        functools.partial(attend_kernel, scale),
        grid=(seqs, heads),
        in_specs=[head, head, head, pl.BlockSpec((1, count * rows, LANES), lambda s, h: (s, 0, 0))],
        out_specs=[head, pl.BlockSpec((1, count, rows), lambda s, h: (s * heads + h, 0, 0))],
        out_shape=[struct(q.shape, BF), struct((seqs * heads, count, rows), F32)],
        compiler_params=params(2),
        cost_estimate=cost(
            2 * seqs * local * (count * rows) ** 2,
            4 * count * seqs * rows * local * 2,
            seqs * heads * (count * rows) ** 2,
        ),
        name="attend",
    )(q, k, v, valid)


def attend_back_kernel(scale, *refs):
    q_ref, k_ref, v_ref, o_ref, lse_ref, valid_ref = refs[:6]
    qr_ref, kr_ref, cos_ref, sin_ref, gq_ref, gk_ref = refs[6:12]
    do_refs = refs[12:-6]
    dq_ref, dk_ref, dv_ref, gains_ref, dk_acc, dv_acc = refs[-6:]
    count, _, rows, width = q_ref.shape
    length = count * rows
    first = jnp.logical_and(pl.program_id(0) == 0, pl.program_id(1) == 0)

    @pl.when(first)
    def _():
        gains_ref[...] = jnp.zeros_like(gains_ref)

    keys = k_ref[...].reshape(length, width)
    keys_t = keys.astype(F32).T.astype(BF)
    values = v_ref[...].reshape(length, width)
    valid = valid_ref[0][:, :1] > 0
    ones = jnp.ones((8, width), F32)

    def back(grad, raw, cos, sin, gain):
        turned = grad * cos - pltpu.roll(grad, LANES // 2, 1) * sin
        scale_rows = rms_scale(raw)
        normed = raw * scale_rows
        scaled = turned * gain
        mean = jnp.mean(scaled * normed, axis=-1, keepdims=True)
        return scale_rows * (scaled - normed * mean), jnp.sum(
            turned * normed, axis=0, keepdims=True
        )

    gain_q = jnp.zeros((1, width), F32)
    gain_k = jnp.zeros((1, width), F32)
    for i in range(count):
        query = q_ref[i, 0]
        grad = do_refs[i][0]
        scores = dot_nt(keys, query) * scale
        weights = jnp.exp(jnp.where(valid, scores, NEG_FILL) - lse_ref[0, i : i + 1, :])
        delta = jnp.sum(
            (grad.astype(F32) * o_ref[i, 0].astype(F32)).T, axis=0, keepdims=True
        )
        d_weights = dot_nt(values, grad)
        d_scores = (weights * (d_weights - delta)).astype(BF)
        dv_part = dot_nn(weights.astype(BF), grad)
        dk_part = dot_nn(d_scores, query)
        if i == 0:
            dv_acc[...] = dv_part
            dk_acc[...] = dk_part
        else:
            dv_acc[...] += dv_part
            dk_acc[...] += dk_part
        dq = (dot_nn(keys_t, d_scores) * scale).T
        d_raw, d_gain = back(dq, qr_ref[i, 0], cos_ref[i], sin_ref[i], gq_ref[...])
        gain_q = gain_q + d_gain
        dq_ref[i, 0] = d_raw.astype(BF)
    for i in range(count):
        dv_ref[i, 0] = dv_acc[i * rows : (i + 1) * rows].astype(BF)
        dk = dk_acc[i * rows : (i + 1) * rows] * scale
        d_raw, d_gain = back(dk, kr_ref[i, 0], cos_ref[i], sin_ref[i], gk_ref[...])
        gain_k = gain_k + d_gain
        dk_ref[i, 0] = d_raw.astype(BF)
    gains_ref[0:1, :] += gain_q
    gains_ref[1:2, :] += gain_k


def attend_back(q, k, v, o, do, lse, valid, q_raw, k_raw, cos, sin, gain_q, gain_k, scale):
    count, seqs, rows, local = q.shape
    heads = local // LANES
    head = pl.BlockSpec((count, 1, rows, LANES), lambda s, h: (0, s, 0, h))
    const = lambda *shape: pl.BlockSpec(shape, lambda s, h: (0,) * len(shape))
    return pl.pallas_call(
        functools.partial(attend_back_kernel, scale),
        grid=(seqs, heads),
        in_specs=[
            head,
            head,
            head,
            head,
            pl.BlockSpec((1, count, rows), lambda s, h: (s * heads + h, 0, 0)),
            pl.BlockSpec((1, count * rows, LANES), lambda s, h: (s, 0, 0)),
            head,
            head,
            const(count, rows, LANES),
            const(count, rows, LANES),
            const(1, LANES),
            const(1, LANES),
        ]
        + [pl.BlockSpec((1, rows, LANES), lambda s, h: (s, 0, h))] * count,
        out_specs=[head, head, head, const(8, LANES)],
        out_shape=[struct(q.shape, BF)] * 3 + [struct((8, LANES), F32)],
        scratch_shapes=[pltpu.VMEM((count * rows, LANES), F32)] * 2,
        compiler_params=params(2),
        cost_estimate=cost(
            5 * seqs * local * (count * rows) ** 2,
            12 * count * seqs * rows * local * 2,
            seqs * heads * (count * rows) ** 2,
        ),
        name="attend_back",
    )(q, k, v, o, lse, valid, q_raw, k_raw, cos, sin, gain_q, gain_k, *do)


def input_back_kernel(dq_ref, dk_ref, dv_ref, wq_ref, wk_ref, wv_ref, out_ref):
    total = None
    for d_ref, w_ref in ((dq_ref, wq_ref), (dk_ref, wk_ref), (dv_ref, wv_ref)):
        grad = d_ref[0].reshape(out_ref.shape[0], w_ref.shape[1])
        part = dot_nt(grad, w_ref[...])
        total = part if total is None else total + part
    out_ref[...] = total.astype(BF)


def input_back(k, dq, dk, dv, weights):
    _, seqs, per, local = dq.shape
    depth = weights.shape[0]
    rows = seqs * per
    tile = min(512, depth)
    grad = pl.BlockSpec((1, seqs, per, local), lambda t: (k, 0, 0, 0))
    return pl.pallas_call(
        input_back_kernel,
        grid=(depth // tile,),
        in_specs=[grad] * 3
        + [pl.BlockSpec((tile, local), lambda t, j=j: (t, j)) for j in range(3)],
        out_specs=pl.BlockSpec((rows, tile), lambda t: (0, t)),
        out_shape=struct((rows, depth), BF),
        compiler_params=params(1),
        cost_estimate=cost(rows * depth * local * 3 // 16, rows * depth * 2 + depth * local * 6),
        name="input_back",
    )(dq, dk, dv, weights, weights, weights)


def out_kernel(count, tok_ref, *refs):
    ob_refs = refs[:count]
    w_ref, x1_ref = refs[count:]
    local = ob_refs[0].shape[1]
    total = tok_ref[...].astype(F32)
    for s in range(count):
        total = total + dot_nn(ob_refs[s][...], w_ref[0, s * local : (s + 1) * local, :])
    x1_ref[...] = total


def out_project(tok, parts, weights):
    rows, depth = tok.shape
    blocks, full, tile = weights.shape
    count = len(parts)
    return pl.pallas_call(
        functools.partial(out_kernel, count),
        grid=(blocks,),
        in_specs=[pl.BlockSpec((rows, tile), lambda j: (0, j))]
        + [pl.BlockSpec(parts[0].shape, lambda j: (0, 0))] * count
        + [pl.BlockSpec((1, full, tile), lambda j: (j, 0, 0))],
        out_specs=pl.BlockSpec((rows, tile), lambda j: (0, j)),
        out_shape=struct((rows, depth), F32),
        compiler_params=params(1),
        cost_estimate=cost(rows * depth * full, rows * depth * 8 + full * depth * 2),
        name="out_project",
    )(tok, *parts, weights)


def out_back_kernel(db_ref, w_ref, out_ref):
    blocks, _, tile = w_ref.shape
    total = None
    for j in range(blocks):
        part = dot_nt(db_ref[:, j * tile : (j + 1) * tile], w_ref[j])
        total = part if total is None else total + part
    out_ref[0] = total.astype(BF)


def out_back(db, weights, count):
    rows, depth = db.shape
    blocks, full, tile = weights.shape
    local = full // count
    return pl.pallas_call(
        out_back_kernel,
        grid=(count,),
        in_specs=[
            pl.BlockSpec((rows, depth), lambda s: (0, 0)),
            pl.BlockSpec((blocks, local, tile), lambda s: (0, s, 0)),
        ],
        out_specs=pl.BlockSpec((1, rows, local), lambda s: (s, 0, 0)),
        out_shape=struct((count, rows, local), BF),
        compiler_params=params(1),
        cost_estimate=cost(rows * depth * full, rows * depth * 2 + full * depth * 2),
        name="out_back",
    )(db, weights)


def expert_kernel(group, experts, n2_ref, c_ref, keep_ref, router_ref, tile_ref, w_ref, *rest):
    last = group == GROUPS - 1
    wt_ref, grad_in, y_in, dn_in = rest[:4]
    hp_ref, da_ref, du_ref, y_ref, dn_ref, grad_out = rest[-14:-8]
    probs, gates, grads, hp_all, da_all, du_all, full, low = rest[-8:]
    e = pl.program_id(0)
    blocks, _, _, ff, tile = w_ref.shape
    rows = n2_ref.shape[0]
    lane = lax.broadcasted_iota(jnp.int32, (rows, LANES), 1)

    @pl.when(e == 0)
    def _():
        logits = jnp.where(lane < EXPERTS, dot_nn(n2_ref[...], router_ref[...]), NEG_FILL)
        raised = jnp.exp(logits - jnp.max(logits, axis=-1, keepdims=True))
        soft = raised / jnp.sum(raised, axis=-1, keepdims=True)
        probs[...] = soft
        gates[...] = soft * keep_ref[0]
        grads[...] = jnp.zeros_like(grads) if group == 0 else grad_in[...]

    @pl.when(e < experts)
    def _():
        for t in range(3):
            for j in range(blocks):
                full[t, :, j * tile : (j + 1) * tile] = w_ref[j, t, 0]
        here = lane == e + group * experts
        gate = jnp.sum(jnp.where(here, gates[...], 0.0), axis=-1, keepdims=True)
        x = n2_ref[...]
        pre = dot_nt(x, full[0])
        up = dot_nt(x, full[1])
        back = dot_nt(c_ref[...], full[2])
        sig = 1.0 / (1.0 + jnp.exp(-pre))
        act = pre * sig
        hid = act * up
        hp = (hid * gate).astype(BF)
        column = jnp.sum(back * hid, axis=-1, keepdims=True)
        grads[...] += jnp.where(here, column * keep_ref[0], 0.0)
        dh = back * gate
        du = (dh * act).astype(BF)
        da = (dh * up * (sig + act * (1.0 - sig))).astype(BF)
        hp_ref[0] = hp
        da_ref[0] = da
        du_ref[0] = du
        place = pl.ds(pl.multiple_of(e * ff, ff), ff)
        hp_all[:, place] = hp
        da_all[:, place] = da
        du_all[:, place] = du

    @pl.when(e == experts - 1)
    def _():
        if last:
            soft = probs[...]
            gd = grads[...]
            dl = (soft * (gd - jnp.sum(soft * gd, axis=-1, keepdims=True))).astype(BF)
            grad_out[...] = dl
            low[...] = dl
        else:
            grad_out[...] = grads[...]

    @pl.when(e >= experts)
    def _():
        wide = experts * ff
        y = dot_nn(hp_all[...], wt_ref[0, 2].reshape(wide, tile))
        total = dot_nn(da_all[...], wt_ref[0, 0].reshape(wide, tile))
        total = total + dot_nn(du_all[...], wt_ref[0, 1].reshape(wide, tile))
        if last:
            total = total + dot_nt(low[...], tile_ref[...])
        if group > 0:
            y = y + y_in[...].astype(F32)
            total = total + dn_in[...].astype(F32)
        y_ref[...] = y.astype(BF)
        dn_ref[...] = total.astype(BF)


def experts_pass(k, count, group, n2, cot, keep, weights_all, weights, before, kept):
    rows, depth = n2.shape
    blocks, _, experts, ff, tile = weights.shape
    router_col = weights_all.shape[1] // LANES - 1
    const = lambda *shape: pl.BlockSpec(shape, lambda e: (0,) * len(shape))
    near = lambda e: jnp.minimum(e, experts - 1)
    far = lambda e: jnp.maximum(e - experts, 0)
    wide = pl.BlockSpec((1, rows, ff), lambda e: (k, 0, near(e)))
    part = pl.BlockSpec((rows, tile), lambda e: (0, far(e)))
    aliased = list(kept or ())
    grad, *sums = before or (jnp.zeros((8, LANES), F32),)
    return pl.pallas_call(
        functools.partial(expert_kernel, group, experts),
        grid=(experts + blocks,),
        in_specs=[
            const(rows, depth),
            const(rows, depth),
            pl.BlockSpec((1, rows, LANES), lambda e: (k, 0, 0)),
            pl.BlockSpec((depth, LANES), lambda e: (0, router_col)),
            pl.BlockSpec((tile, LANES), lambda e: (far(e), router_col)),
            pl.BlockSpec((blocks, 3, 1, ff, tile), lambda e: (0, 0, near(e), 0, 0)),
            pl.BlockSpec((1, 3, experts, ff, tile), lambda e: (far(e), 0, 0, 0, 0)),
            const(*grad.shape),
        ]
        + [part] * len(sums)
        + [pl.BlockSpec(memory_space=pl.ANY)] * len(aliased),
        out_specs=[wide, wide, wide, part, part, const(rows, LANES)],
        out_shape=[struct((count, rows, experts * ff), BF)] * 3
        + [struct((rows, depth), BF)] * 2
        + [struct((rows, LANES), BF if group == GROUPS - 1 else F32)],
        input_output_aliases={8 + len(sums) + i: i for i in range(len(aliased))},
        scratch_shapes=[pltpu.VMEM((rows, LANES), F32)] * 3
        + [pltpu.VMEM((rows, experts * ff), BF)] * 3
        + [pltpu.VMEM((3, ff, depth), BF), pltpu.VMEM((rows, LANES), BF)],
        compiler_params=params(1),
        cost_estimate=cost(
            6 * rows * depth * ff * experts,
            6 * experts * depth * ff * 2 + 4 * rows * depth * 2 + 3 * rows * experts * ff * 2,
            2 * rows * ff * experts,
        ),
        name=f"experts_{group}",
    )(n2, cot, keep, weights_all, weights_all, weights, weights, grad, *sums, *aliased)


def row_grad_kernel(count, plan, router, gain, shared, *refs):
    ins = list(refs)
    lefts, rights = [], []
    for parts, tiles in plan:
        lefts.append([ins.pop(0) for _ in range(parts)])
        rights.append([ins.pop(0) for _ in tiles])
    dls = [ins.pop(0) for _ in range(count)] if router else []
    weight_ref = ins.pop(0) if gain else None
    if shared:
        ins.pop(0)
    out_ref, extra_ref, turned = ins.pop(0), ins.pop(0) if router or gain else None, ins.pop(0)
    i = pl.program_id(0)
    start = 0
    for (parts, tiles), left, right in zip(plan, lefts, rights):
        rows = left[0].shape[0]

        @pl.when(i == start)
        def _():
            for k in range(parts):
                turned[:, k * rows : (k + 1) * rows] = left[k][...].T
            if router and start == 0:
                total = None
                for k in range(count):
                    part = dot_nn(turned[:, k * rows : (k + 1) * rows], dls[k][...])
                    total = part if total is None else total + part
                extra_ref[...] = total
            if gain:
                extra_ref[...] = jnp.zeros_like(extra_ref)

        for ref, steps in zip(right, tiles):

            @pl.when(jnp.logical_and(i >= start, i < start + steps))
            def _():
                tile = out_ref.shape[1]
                full = dot_nn(turned[:, : parts * rows], ref[...].reshape(parts * rows, tile))
                out_ref[...] = full.astype(BF)
                if gain:
                    product = full * weight_ref[...].astype(F32)
                    for j in range(tile // LANES):
                        extra_ref[...] += product[:, j * LANES : (j + 1) * LANES]

            start += steps


def row_grads(pairs, tile, name, dls=(), weights=None, total=None, base=None):
    plan, args, specs, start, macs = [], [], [], 0, 0
    depth = pairs[0][0][0].shape[1]
    most = max(sum(part.shape[0] for part in left) for left, _ in pairs)

    def piece(array, first, steps):
        lead = array.shape[:-1]
        return pl.BlockSpec(
            lead + (tile,),
            lambda i: (0,) * len(lead) + (jnp.clip(i - first, 0, steps - 1),),
        )

    whole = pl.Buffered(1)
    for left, right in pairs:
        args += left
        specs += [pl.BlockSpec(p.shape, lambda i: (0, 0), pipeline_mode=whole) for p in left]
        tiles = []
        for array in right:
            steps = array.shape[-1] // tile
            args.append(array)
            specs.append(piece(array, start, steps))
            tiles.append(steps)
            start += steps
            macs += len(left) * left[0].shape[0] * depth * steps * tile
        plan.append((len(left), tuple(tiles)))
    wide = base.shape[1] if base is not None else total or start * tile
    skip = wide // tile - start if base is not None else 0
    out_specs = [pl.BlockSpec((depth, tile), lambda i: (0, i + skip))]
    out_shape = [struct((depth, wide), BF)]
    if dls:
        args += dls
        specs += [pl.BlockSpec(d.shape, lambda i: (0, 0)) for d in dls]
    if weights is not None:
        args.append(weights)
        specs.append(pl.BlockSpec((depth, tile), lambda i: (0, i)))
    if base is not None:
        args.append(base)
        specs.append(pl.BlockSpec(memory_space=pl.ANY))
    if dls or weights is not None:
        out_specs.append(pl.BlockSpec((depth, LANES), lambda i: (0, 0)))
        out_shape.append(struct((depth, LANES), F32))
    return pl.pallas_call(
        functools.partial(
            row_grad_kernel,
            len(dls),
            tuple(plan),
            bool(dls),
            weights is not None,
            base is not None,
        ),
        grid=(start,),
        in_specs=specs,
        out_specs=out_specs,
        out_shape=out_shape,
        scratch_shapes=[pltpu.VMEM((depth, most), BF)],
        input_output_aliases={} if base is None else {len(args) - 1: 0},
        compiler_params=params(1),
        cost_estimate=cost(macs if 'experts' in name else macs // 16, 2 * depth * start * tile + 4 * most * depth),
        name=name,
    )(*args)


def per_device(
    tokens,
    lengths,
    routes,
    slot_order,
    attn_gain,
    query_gain,
    key_gain,
    query_weight,
    key_weight,
    value_weight,
    out_weight,
    moe_gain,
    router_weight,
    gate_weight,
    up_weight,
    down_weight,
    cotangent,
):
    per, seqs, depth = tokens.shape
    count = lax.axis_size("tp")
    me = lax.axis_index("tp")
    length = per * count
    rows = seqs * per
    head_width = query_gain.shape[0]
    local = query_weight.shape[1]
    scale = head_width ** (-0.5)

    first = jnp.concatenate(
        [
            query_weight,
            key_weight,
            value_weight,
            jnp.pad(router_weight, ((0, 0), (0, LANES - EXPERTS))),
        ],
        axis=1,
    )
    weights_all = lax.all_gather(first, "fsdp", axis=0, tiled=True)

    tok = jnp.transpose(tokens, (1, 0, 2)).reshape(rows, depth)
    tok_float = tok.astype(F32)
    n1_own = (tok_float * rms_scale(tok_float) * attn_gain).astype(BF)
    outs = exchange([after(out_weight, n1_own)] * count, -1)
    n1 = [n1_own, shift(after(n1_own, *outs[1:]), count, 1)]
    own_pos = me * per + jnp.arange(per, dtype=jnp.int32)
    valid_own = own_pos[None, :] < lengths[:, None]
    route_t = jnp.transpose(routes, (2, 1, 0)).reshape(TOP, rows)
    order_t = jnp.transpose(slot_order, (2, 1, 0)).reshape(TOP, rows)
    names = jnp.arange(EXPERTS, dtype=jnp.int32)[:, None]
    order_own = jnp.full((EXPERTS, rows), FAR, jnp.int32)
    for j in range(TOP):
        order_own = jnp.where(route_t[j][None, :] == names, order_t[j][None, :], order_own)
    order_own = jnp.where(valid_own.reshape(1, rows), order_own, FAR)
    orders = exchange([after(order_own, n1[1])] * count, 1)

    each = EXPERTS // GROUPS
    gather = lambda value: lax.all_gather(value, "fsdp", axis=0, tiled=False)

    def group_weights(g):
        part = slice(g * each, (g + 1) * each)
        stacked = jnp.concatenate(
            [
                jnp.swapaxes(gate_weight[part], 1, 2),
                jnp.swapaxes(up_weight[part], 1, 2),
                down_weight[part],
            ]
        )
        stacked = after(stacked, weights_all, n1[1])
        return gather(stacked.reshape((3, each) + stacked.shape[1:]))

    out_all = gather(jnp.concatenate(outs, axis=0))
    moe_weights = [group_weights(g) for g in range(GROUPS)]
    owner = (me - jnp.arange(count, dtype=jnp.int32)) % count
    chunk_pos = owner[:, None] * per + jnp.arange(per, dtype=jnp.int32)[None, :]
    half = head_width // 2
    frequency = ROPE_BASE ** (-(jnp.arange(half, dtype=F32) * 2.0 / head_width))
    angles = chunk_pos.astype(F32)[:, :, None] * frequency
    cos_half, sin_half = jnp.cos(angles), jnp.sin(angles)
    cos = jnp.concatenate([cos_half, cos_half], axis=-1)
    sin = jnp.concatenate([-sin_half, sin_half], axis=-1)
    key_valid = (chunk_pos.reshape(1, length) < lengths[:, None]).astype(F32)
    key_valid = jnp.broadcast_to(key_valid[:, :, None], (seqs, length, LANES))

    gain_q, gain_k = query_gain[None, :], key_gain[None, :]
    kept, done = None, []
    for k in range(count):
        if k > 1:
            n1.append(shift(after(n1[-1], *(done[: k - 1] if k > 2 else ())), count, 1))
        kept = project(
            k, count, seqs, after(n1[k], *done[-1:]), weights_all, cos, sin, gain_q, gain_k, kept
        )
        done.append(kept[4])
    q_raw, k_raw, q, k_low, v = kept
    keep = keep_rows(after(jnp.stack(orders), done[1]), length * seqs * TOP)

    cot = jnp.transpose(cotangent, (1, 0, 2)).reshape(rows, depth)
    cot_own = jnp.where(valid_own.reshape(rows, 1), cot, jnp.zeros_like(cot))
    cots = [cot_own, shift(after(cot_own, n1[-1], done[count - 2]), count, 1)]

    ob, lse = attend(q, k_low, v, key_valid, scale)
    ob_rows = after(ob.reshape(count, rows, local), cots[1])
    ob_parts = exchange(ob_rows, -1)
    x1 = out_project(tok, ob_parts, out_all)
    n2_own = (x1 * rms_scale(x1) * moe_gain).astype(BF)
    n2 = [n2_own, shift(n2_own, count, 1)]
    token = [n2_own]

    bufs = [None] * GROUPS
    ys, dns, grads = [None] * count, [None] * count, [None] * count

    def run(group, k):
        before = (grads[k], ys[k], dns[k]) if group else None
        hp, da, du, ys[k], dns[k], grads[k] = experts_pass(
            k, count, group, after(n2[k], *token), cots[k], keep, weights_all, moe_weights[group],
            before, bufs[group],
        )
        bufs[group] = (hp, da, du)
        token[0] = dns[k]
        return dns[k]

    def next_inputs(done):
        if len(n2) < count:
            n2.append(shift(after(n2[-1], done), count, 1))
        if len(cots) < count:
            cots.append(shift(after(cots[-1], done), count, 1))

    ready = run(0, 0)
    next_inputs(ready)
    run(0, 1)
    ready = run(1, 0)
    next_inputs(ready)
    for k in range(2, count):
        run(0, k)
        if k < count - 1:
            next_inputs(run(1, k - 1))
    dn_run = shift(dns[1], count, 1)
    token.append(dn_run)
    y_run = shift(after(ys[1], dns[count - 1]), count, 1)
    ff = gate_weight.shape[2]
    hp, da, du = bufs[0]
    first_full = row_grads(
        [([after(n2[0], *token)] + n2[1:], [da, du]), (cots, [hp])], ff, "experts_first_grads"
    )[0]
    first_own = lax.psum_scatter(first_full, "fsdp", scatter_dimension=0, tiled=True)
    token = [first_full, y_run]
    run(1, count - 2)
    for k in range(2, count):
        dn_run = plus(dn_run, dns[k]).astype(BF)
        token.append(dn_run)
        if k == count - 2:
            run(1, count - 1)
        dn_run = shift(dn_run, count, 1)
    hp, da, du = bufs[1]
    last_full, router_term = row_grads(
        [([after(n2[0], *token)] + n2[1:], [da, du])], ff, "experts_last_grads", grads
    )
    dn2 = plus(after(dn_run, last_full), dns[0])


    moe_back, moe_gain_term = norm_back(dn2, x1, moe_gain)
    dx1 = moe_back + cot_own.astype(F32)
    db = dx1.astype(BF)
    dob = out_back(db, out_all, count)
    last_own = lax.psum_scatter(after(last_full, dob), "fsdp", scatter_dimension=0, tiled=True)
    dob = after(dob, first_own)
    dob_parts = exchange(dob, 1)
    y_sum = plus(after(y_run, dob), ys[2]).astype(BF)
    rest_full = row_grads(
        [(cots, [hp]), ([after(db, dob)], ob_parts)],
        ff, "rest_grads",
    )[0]
    d_ob = [after(part.reshape(seqs, per, local), rest_full, y_sum) for part in dob_parts]
    rest_own = lax.psum_scatter(after(rest_full, *d_ob), "fsdp", scatter_dimension=0, tiled=True)
    y_run = shift(after(y_sum, *d_ob), count, 1)
    for k in range(3, count - 1):
        y_run = shift(plus(y_run, ys[k]).astype(BF), count, 1)

    dq, dk, dv, gains = attend_back(
        q, k_low, v, ob, d_ob, lse, key_valid, q_raw, k_raw, cos, sin, gain_q, gain_k, scale
    )
    part = input_back(1, after(dq, y_run), dk, dv, weights_all)
    dn1_run = shift(part, count, 1)
    attn_full, attn_gain_wide = row_grads(
        [([after(n1[0], part)] + n1[1:], [a.reshape(count * rows, local) for a in (dq, dk, dv)])],
        min(256, local), "qkv_grads", weights=weights_all,
    )

    attn_own = lax.psum_scatter(attn_full, "fsdp", scatter_dimension=0, tiled=True)

    attn_gain_term = jnp.sum(attn_gain_wide, axis=1) / attn_gain
    packed = jnp.concatenate(
        [router_term[:, :EXPERTS].reshape(-1, LANES)]
        + [v.reshape(-1, LANES) for v in (attn_gain_term, moe_gain_term, gains[:2])],
        axis=0,
    )
    bits = [1 << b for b in range(count.bit_length() - 1)]
    across = lambda value, axis, bit: value + lax.ppermute(
        value, axis, [(i, i ^ bit) for i in range(lax.axis_size(axis))]
    )

    part = input_back(2, after(dq, attn_full), dk, dv, weights_all)
    dn1_run = after(dn1_run, last_own)
    for k in range(2, count):
        dn1_run = plus(dn1_run, part).astype(BF)
        if k == 2:
            packed = after(packed, dn1_run)
            for b in range(lax.axis_size("fsdp").bit_length() - 1):
                packed = across(packed, "fsdp", 1 << b)
        elif bits:
            packed = across(after(packed, dn1_run), "tp", bits.pop())
        dn1_run = shift(dn1_run, count, 1)
        part = input_back((k + 1) % count, dq, dk, dv, weights_all)
    packed = after(packed, dn1_run)
    while bits:
        packed = across(packed, "tp", bits.pop())
    dn1 = plus(dn1_run, part)
    y_run = shift(plus(after(y_run, dn1_run, rest_own), ys[count - 1]).astype(BF), count, 1)
    out_own = rest_own[:, each * ff :]
    out_pieces = [out_own[:, s * local : (s + 1) * local] for s in range(count)]
    out_pieces = exchange(out_pieces, 1)
    out_weight_grad = jnp.transpose(plus(*out_pieces))

    def expert_out(owns, axes):
        shaped = [own.reshape(own.shape[0], each, ff) for own in owns]
        return jnp.concatenate([jnp.transpose(v, axes) for v in shaped], axis=0).astype(F32)

    wide = each * ff
    gate_grad = expert_out((first_own[:, :wide], last_own[:, :wide]), (1, 0, 2))
    up_grad = expert_out((first_own[:, wide : 2 * wide], last_own[:, wide:]), (1, 0, 2))
    down_grad = expert_out((first_own[:, 2 * wide :], rest_own[:, :wide]), (1, 2, 0))

    attn_back = norm_back(dn1, tok_float, attn_gain)[0]
    tokens_grad = attn_back + dx1
    y_run = after(y_run, tokens_grad, out_weight_grad)
    layer_out = (x1 + plus(y_run, ys[0])).astype(BF)
    layer_out = jnp.transpose(layer_out.reshape(seqs, per, depth), (1, 0, 2))
    qkv_sum = after(attn_own, layer_out, out_weight_grad, packed).astype(F32)

    split = depth * EXPERTS // LANES
    across = depth // LANES
    small = (
        packed[split : split + across].reshape(depth),
        packed[split + 2 * across],
        packed[split + 2 * across + 1],
        packed[split + across : split + 2 * across].reshape(depth),
        packed[:split].reshape(depth, EXPERTS),
    )
    router_rows = depth // lax.axis_size("fsdp")
    router_grad = lax.dynamic_slice_in_dim(
        small[4], lax.axis_index("fsdp") * router_rows, router_rows, 0
    )

    def back_to_positions(value):
        return jnp.transpose(value.reshape(seqs, per, depth), (1, 0, 2))

    return (
        layer_out,
        back_to_positions(tokens_grad),
        small[0],
        small[1],
        small[2],
        qkv_sum[:, :local],
        qkv_sum[:, local : 2 * local],
        qkv_sum[:, 2 * local :],
        out_weight_grad,
        small[3],
        router_grad,
        gate_grad,
        up_grad,
        down_grad,
    )


def solution(mesh):
    return jax.shard_map(
        per_device,
        mesh=mesh,
        in_specs=(
            P("tp", "fsdp", None),
            P("fsdp"),
            P("tp", "fsdp", None),
            P("tp", "fsdp", None),
            P(),
            P(),
            P(),
            P("fsdp", "tp"),
            P("fsdp", "tp"),
            P("fsdp", "tp"),
            P("tp", "fsdp"),
            P(),
            P("fsdp", None),
            P(None, "fsdp", "tp"),
            P(None, "fsdp", "tp"),
            P(None, "tp", "fsdp"),
            P("tp", "fsdp", None),
        ),
        out_specs=(
            P("tp", "fsdp", None),
            P("tp", "fsdp", None),
            P(),
            P(),
            P(),
            P("fsdp", "tp"),
            P("fsdp", "tp"),
            P("fsdp", "tp"),
            P("tp", "fsdp"),
            P(),
            P("fsdp", None),
            P(None, "fsdp", "tp"),
            P(None, "fsdp", "tp"),
            P(None, "tp", "fsdp"),
        ),
        check_vma=False,
    )
```
